128 devices in a mesh: ka: 4 (over x_hi, core), band: 32 (over y, x_lo, z).
Axes of the slice: x: 4 (x_hi: 2, x_lo: 2; x = x_hi * 2 + x_lo), y: 4, z: 4, core: 2. Of those that a mesh axis runs over, the one named last changes fastest.
Arguments:
- occ_orb: float32 [8, 64, 2, 4096], P('ka'), may hold values from -6 to 6
- occ_energy: float32 [8, 64], P('ka'), may hold values from -6 to -0.5
- emp_orb: float32 [8, 64, 2, 4096], P('ka', 'band'), may hold values from -6 to 6
- emp_energy: float32 [8, 64], P('ka', 'band'), may hold values from 0.5 to 8
- gidx: int32 [2048], replicated, may hold values from 0 to 4095, as said below
- sym_map: int32 [8, 2048], P('ka'), may hold values from 0 to 2047, as said below
- weights: int32 [8], replicated, may hold values from 1 to 8
- count: int32 [8], replicated, may hold values from 16 to 64, as said below
Outputs:
- chi_rows: float32 [1, 1024, 2, 2048], P(None, ('ka', 'band'))
The draws below stay inside these ranges and needn't reach their ends.
Inputs may be any that keep to these rules, and one draw needn't show every extreme that they name: `gidx`: distinct values; 0 and 4095 are among them. `sym_map`: each row is a permutation of 0 to 2047. `count`: some k point has all 64 empty bands, another has 16.
All inputs are finite; a program needn't handle non-finite values.
Results may differ from the reference program's by a relative error of at most 0.0003.
Values sent between devices are 32-bit elements; how exact they have to be, the bound alone decides.
No kernel may reach another device: no remote copies, remote signals or barrier semaphores. Data moves between devices by JAX's collectives and lax.ppermute only.
A program may use at most 128 MiB of HBM per device.

```python
import jax
import jax.numpy as jnp
from jax import lax

GA = 16
GB = 16
GC = 16
NG = 2048
NGC = 1024
VB = 64
NQ = 1
NK = 8
EMPTY = 64
R = 4096


def draw_gidx(key, part):
    key = jax.random.fold_in(key, 11)
    first_key, second_key = jax.random.split(key)
    points = GA * GB * GC
    inner = 1 + jax.random.permutation(first_key, points - 2)[:NG - 2]
    chosen = jnp.concatenate([jnp.array([0, points - 1], jnp.int32), inner.astype(jnp.int32)])
    order = jax.random.permutation(second_key, NG)
    return chosen[order].astype(jnp.int32)


def draw_sym_map(key, part):
    key = jax.random.fold_in(key, 12)
    row_keys = jax.random.split(key, NK)
    rows = jax.vmap(lambda single: jax.random.permutation(single, NG))(row_keys)
    return rows.astype(jnp.int32)


def draw_count(key, part):
    key = jax.random.fold_in(key, 13)
    base_key, top_key, low_key = jax.random.split(key, 3)
    base = jax.random.randint(base_key, (NK,), EMPTY // 4, EMPTY + 1)
    top = jax.random.randint(top_key, (), 0, NK)
    lowest = (top + 1 + jax.random.randint(low_key, (), 0, NK - 1)) % NK
    base = base.at[top].set(EMPTY).at[lowest].set(EMPTY // 4)
    return base.astype(jnp.int32)


def touch_ends(values, own_key, low, top_value):
    extent = values.shape
    spot = [jax.random.randint(jax.random.fold_in(own_key, axis), (), 0, extent[axis]) for axis in range(len(extent))]
    values = values.at[tuple(spot)].set(low)
    longest = extent.index(max(extent))
    spot[longest] = (spot[longest] + 1) % extent[longest]
    return values.at[tuple(spot)].set(top_value)


def shard_levels(rng, shape, cuts, least, top_value):
    gain, own = 1.0, jax.random.fold_in(rng, 6)
    for position, blocks in cuts:
        heights = jnp.exp(jax.random.uniform(jax.random.fold_in(own, position), (blocks,), jnp.float32, least / len(cuts), top_value / len(cuts)))
        gain = gain * jnp.repeat(heights, shape[position] // blocks).reshape([-1 if axis == position else 1 for axis in range(len(shape))])
    return gain


def centred(key, extent, deviation, bound, cuts=(), kind=jnp.bfloat16):
    values = deviation * jax.random.normal(key, extent, jnp.float32)
    if cuts:
        values = values * shard_levels(key, extent, cuts, -0.22, 0.18)
    return jnp.clip(values, -bound, bound).astype(kind)


def setup_inputs(seed: int = 0) -> dict:
    arg_keys = jax.random.split(jax.random.key(seed), 9)
    return {
        "occ_orb": centred(arg_keys[0], (NK, VB, 2, R), 1.0, 6.0, ((0, 4),), jnp.float32),
        "occ_energy": jnp.clip(-6.0 + 5.5 * jax.random.uniform(arg_keys[1], (NK, VB), jnp.float32) ** shard_levels(arg_keys[1], (NK, VB), ((0, 4),), -0.2, 0.2), -6.0, -0.5),
        "emp_orb": centred(arg_keys[2], (NK, EMPTY, 2, R), 1.0, 6.0, ((0, 4), (1, 32)), jnp.float32),
        "emp_energy": jnp.clip(0.5 + 7.5 * jax.random.uniform(arg_keys[3], (NK, EMPTY), jnp.float32) ** shard_levels(arg_keys[3], (NK, EMPTY), ((0, 4), (1, 32)), -0.2, 0.2), 0.5, 8.0),
        "gidx": draw_gidx(jax.random.fold_in(arg_keys[8], 71), 0),
        "sym_map": draw_sym_map(jax.random.fold_in(arg_keys[8], 71), 0),
        "weights": touch_ends(jax.random.randint(arg_keys[6], (NK,), 1, 9), jax.random.fold_in(arg_keys[6], 1), 1, 8).astype(jnp.int32),
        "count": draw_count(jax.random.fold_in(arg_keys[8], 71), 0),
    }


def reference(occ_orb, occ_energy, emp_orb, emp_energy, gidx, sym_map, weights, count):
    points = GA * GB * GC
    plane = GB * GC
    wsum = jnp.sum(weights).astype(jnp.float32)
    scale = -4.0 / jnp.sqrt(jnp.float32(VB * EMPTY) * wsum)
    band_line = jnp.arange(EMPTY, dtype=jnp.int32)
    results = []
    for step in range(1, NQ + 1):

        def one_k(total, kpoint):
            raw = kpoint + step
            wrapped = (raw >= NK).astype(jnp.int32)
            target = raw - wrapped * NK
            occ = occ_orb[kpoint]
            emp = emp_orb[target]
            real_pair = occ[:, None, 0, :] * emp[None, :, 0, :] + occ[:, None, 1, :] * emp[None, :, 1, :]
            imag_pair = occ[:, None, 0, :] * emp[None, :, 1, :] - occ[:, None, 1, :] * emp[None, :, 0, :]
            field = (real_pair + 1j * imag_pair).reshape(VB * EMPTY, GA, GB, GC)
            spectrum = jnp.fft.fftn(field, axes=(1, 2, 3)).reshape(VB * EMPTY, points) / jnp.sqrt(jnp.float32(points))
            index = ((gidx[sym_map[kpoint]] + wrapped * plane) % points).astype(jnp.int32)
            dens_real = jnp.take(jnp.real(spectrum), index, axis=1).astype(jnp.float32)
            dens_imag = jnp.take(jnp.imag(spectrum), index, axis=1).astype(jnp.float32)
            live = (band_line < count[target]).astype(jnp.float32)
            gap = emp_energy[target][None, :] - occ_energy[kpoint][:, None]
            factor = (scale * weights[kpoint].astype(jnp.float32) * live[None, :] / gap).reshape(VB * EMPTY)
            left_real = dens_real[:, :NGC] * factor[:, None]
            left_imag = dens_imag[:, :NGC] * factor[:, None]
            hp = lax.Precision.HIGHEST
            part_real = jnp.dot(left_real.T, dens_real, precision=hp) + jnp.dot(left_imag.T, dens_imag, precision=hp)
            part_imag = jnp.dot(left_real.T, dens_imag, precision=hp) - jnp.dot(left_imag.T, dens_real, precision=hp)
            return (total + jnp.stack([part_real, part_imag], axis=1), None)
        start = jnp.zeros((NGC, 2, NG), jnp.float32)
        total, unused = lax.scan(one_k, start, jnp.arange(NK, dtype=jnp.int32))
        results.append(total)
    return jnp.stack(results, axis=0)
```

```python
import functools

import jax
import jax.numpy as jnp
import numpy as np
from jax import lax
from jax.experimental import pallas as pl
from jax.experimental.pallas import tpu as pltpu
from jax.sharding import PartitionSpec as P

GRID = 16
PLANE = GRID * GRID
POINTS = GRID * PLANE
HALF = PLANE // 2
NG = 2048
VB = 64
KA = 4
BAND = 32
YS = 4
MEMBERS = BAND // YS
CHUNK = 2 * VB
KLOC = 2
DEPTH = KLOC * YS * 2 * CHUNK
ROWS = 256
LINES = POINTS // 128


def plane_matrices():
    point = np.arange(HALF)
    outer, inner = point // GRID, point % GRID
    parts = []
    for parity in range(2):
        turns = np.outer(2 * outer + parity, outer) + np.outer(inner, inner)
        angle = 2.0 * np.pi * (turns % GRID) / GRID
        cos, sin = np.cos(angle), np.sin(angle)
        parts.append(np.block([[cos, sin], [-sin, cos]]))
    whole = np.stack(parts).astype(np.float32)
    high = whole.astype(jnp.bfloat16)
    low = (whole - high.astype(np.float32)).astype(jnp.bfloat16)
    return high, low


def split(value):
    high = value.astype(jnp.bfloat16)
    low = (value - high.astype(jnp.float32)).astype(jnp.bfloat16)
    return high, low


def four(points):
    (ar, ai), (br, bi), (cr, ci), (dr, di) = points
    sr, si = ar + cr, ai + ci
    tr, ti = ar - cr, ai - ci
    ur, ui = br + dr, bi + di
    wr, wi = br - dr, bi - di
    return [(sr + ur, si + ui), (tr + wi, ti - wr), (sr - ur, si - ui), (tr - wi, ti + wr)]


def turned(point, power):
    re, im = point
    power %= GRID
    if power == 0:
        return re, im
    if power == 4:
        return im, -re
    if power == 2:
        root = float(np.sqrt(0.5))
        return (re + im) * root, (im - re) * root
    if power == 6:
        root = float(np.sqrt(0.5))
        return (im - re) * root, (re + im) * -root
    cos = float(np.cos(2 * np.pi * power / GRID))
    sin = float(np.sin(2 * np.pi * power / GRID))
    return re * cos + im * sin, im * cos - re * sin


def dot_t(left, right):
    return lax.dot_general(left, right, (((1,), (1,)), ((), ())), preferred_element_type=jnp.float32)


def kernel(
    place_ref, sym_ref, rows_ref, occ_ref, emp_ref, fac_ref, whi_ref, wlo_ref, near_ref, far_ref,
    mid_ref, xhi_ref, xlo_ref, spec_ref, dens_ref, bhi_ref, blo_ref, ahi_ref, alo_ref,
):
    def one_k(k, carry):
        def one_chunk(chunk, carry):
            def one_block(block, carry):
                band = block // (VB // 16)
                start = pl.multiple_of((block % (VB // 16)) * 16, 16)
                line = k * (2 * YS) + chunk * 2 + band

                def pair(a, half):
                    base = a * PLANE + half * HALF
                    o_re = occ_ref[k, 0, pl.ds(start, 16), pl.ds(base, HALF)]
                    o_im = occ_ref[k, 1, pl.ds(start, 16), pl.ds(base, HALF)]
                    at = a * 2 + half
                    e_re = emp_ref[line, at : at + 1, :]
                    e_im = emp_ref[line, LINES + at : LINES + at + 1, :]
                    return o_re * e_re + o_im * e_im, o_re * e_im - o_im * e_re

                for a0 in range(4):
                    even, odd = [], []
                    for a1 in range(4):
                        fr, fi = pair(4 * a1 + a0, 0)
                        sr, si = pair(4 * a1 + a0, 1)
                        even.append((fr + sr, fi + si))
                        odd.append((fr - sr, fi - si))
                    for parity, points in enumerate((even, odd)):
                        for k0, point in enumerate(four(points)):
                            re, im = turned(point, a0 * k0)
                            mid_ref[parity, k0, a0, 0] = re
                            mid_ref[parity, k0, a0, 1] = im
                row = pl.multiple_of(block * 16, 16)
                for parity in range(2):
                    for k0 in range(4):
                        points = [(mid_ref[parity, k0, a0, 0], mid_ref[parity, k0, a0, 1]) for a0 in range(4)]
                        for k1, point in enumerate(four(points)):
                            at = k0 + 4 * k1
                            for part in range(2):
                                high, low = split(point[part])
                                xhi_ref[parity, pl.ds(at * CHUNK + row, 16), pl.ds(part * HALF, HALF)] = high
                                xlo_ref[parity, pl.ds(at * CHUNK + row, 16), pl.ds(part * HALF, HALF)] = low
                return carry

            lax.fori_loop(0, CHUNK // 16, one_block, 0)

            def one_tile(tile, carry):
                for parity in range(2):
                    at = pl.ds(pl.multiple_of(tile * 2 * CHUNK, 2 * CHUNK), 2 * CHUNK)
                    xhi = xhi_ref[parity, at, :]
                    xlo = xlo_ref[parity, at, :]
                    whi = whi_ref[parity]
                    out = dot_t(whi, xhi) + dot_t(whi, xlo) + dot_t(wlo_ref[parity], xhi)
                    for which in range(2):
                        base = ((tile * 2 + which) * PLANE + parity * HALF) * 8 + chunk * 2
                        for part in range(2):
                            spec_ref[pl.ds(base + part, HALF, stride=8), :] = out[
                                part * HALF : (part + 1) * HALF, which * CHUNK : (which + 1) * CHUNK
                            ]
                return carry

            lax.fori_loop(0, GRID // 2, one_tile, 0)
            return carry

        lax.fori_loop(0, YS, one_chunk, 0)

        shift = rows_ref[ROWS // 8 + k]

        def gathered(count, row_of):
            def sixteen(step, carry):
                for lane in range(16):
                    at = step * 16 + lane
                    source = (place_ref[sym_ref[k, row_of(at)]] + shift) & (POINTS * 8 - 1)
                    source = pl.multiple_of(source, 8)
                    dens_ref[pl.ds(pl.multiple_of(at * 8, 8), 8), :] = spec_ref[pl.ds(source, 8), :]
                return carry

            lax.fori_loop(0, count // 16, sixteen, 0)

        def columns(slot):
            return pl.ds(pl.multiple_of(k * (8 * CHUNK) + slot * CHUNK, CHUNK), CHUNK)

        gathered(ROWS, lambda at: rows_ref[at // 8] + at % 8)

        def left(step, carry):
            row = pl.multiple_of(step * 16, 16)
            for chunk in range(YS):
                factor = fac_ref[pl.ds(k * YS + chunk, 1), :]
                re = dens_ref[pl.ds(row * 8 + 2 * chunk, 16, stride=8), :] * factor
                im = dens_ref[pl.ds(row * 8 + 2 * chunk + 1, 16, stride=8), :] * factor
                rhi, rlo = split(re)
                ihi, ilo = split(im)
                ahi_ref[pl.ds(row, 16), columns(2 * chunk)] = rhi
                alo_ref[pl.ds(row, 16), columns(2 * chunk)] = rlo
                ahi_ref[pl.ds(row, 16), columns(2 * chunk + 1)] = ihi
                alo_ref[pl.ds(row, 16), columns(2 * chunk + 1)] = ilo
                ahi_ref[pl.ds(ROWS + row, 16), columns(2 * chunk)] = -ihi
                alo_ref[pl.ds(ROWS + row, 16), columns(2 * chunk)] = -ilo
                ahi_ref[pl.ds(ROWS + row, 16), columns(2 * chunk + 1)] = rhi
                alo_ref[pl.ds(ROWS + row, 16), columns(2 * chunk + 1)] = rlo
            return carry

        lax.fori_loop(0, ROWS // 16, left, 0)
        gathered(NG, lambda at: at)

        def right(step, carry):
            row = pl.multiple_of(step * 16, 16)
            for slot in range(8):
                high, low = split(dens_ref[pl.ds(row * 8 + slot, 16, stride=8), :])
                bhi_ref[pl.ds(row, 16), columns(slot)] = high
                blo_ref[pl.ds(row, 16), columns(slot)] = low
            return carry

        lax.fori_loop(0, NG // 16, right, 0)
        return carry

    lax.fori_loop(0, KLOC, one_k, 0)

    def one_column(tile, carry):
        at = pl.ds(pl.multiple_of(tile * 256, 256), 256)
        bhi = bhi_ref[at, :]
        blo = blo_ref[at, :]
        ahi = ahi_ref[...]
        out = dot_t(ahi, bhi) + dot_t(ahi, blo) + dot_t(alo_ref[...], bhi)
        for part in range(2):
            near_ref[part, :, at] = out[part * ROWS : part * ROWS + ROWS // 2]
            far_ref[part, :, at] = out[part * ROWS + ROWS // 2 : (part + 1) * ROWS]
        return carry

    lax.fori_loop(0, NG // 256, one_column, 0)


def partial_rows(places, sym_map, rows, occ, emp, factor):
    whi, wlo = plane_matrices()
    vmem = pl.BlockSpec(memory_space=pltpu.VMEM)
    smem = pl.BlockSpec(memory_space=pltpu.SMEM)
    part = jax.ShapeDtypeStruct((2, ROWS // 2, NG), jnp.float32)
    return pl.pallas_call(
        kernel,
        out_shape=(part, part),
        in_specs=[smem, smem, smem, vmem, vmem, vmem, vmem, vmem],
        out_specs=(vmem, vmem),
        scratch_shapes=[
            pltpu.VMEM((2, 4, 4, 2, 16, HALF), jnp.float32),
            pltpu.VMEM((2, GRID * CHUNK, PLANE), jnp.bfloat16),
            pltpu.VMEM((2, GRID * CHUNK, PLANE), jnp.bfloat16),
            pltpu.VMEM((POINTS * 8, CHUNK), jnp.float32),
            pltpu.VMEM((NG * 8, CHUNK), jnp.float32),
            pltpu.VMEM((NG, DEPTH), jnp.bfloat16),
            pltpu.VMEM((NG, DEPTH), jnp.bfloat16),
            pltpu.VMEM((2 * ROWS, DEPTH), jnp.bfloat16),
            pltpu.VMEM((2 * ROWS, DEPTH), jnp.bfloat16),
        ],
        compiler_params=pltpu.CompilerParams(vmem_limit_bytes=62 * 2**20),
        cost_estimate=pl.CostEstimate(flops=40 * 10**9, bytes_accessed=10 * 2**20, transcendentals=0),
    )(places, sym_map, rows, occ, emp, factor, jnp.asarray(whi), jnp.asarray(wlo))


def place(index):
    ka, band = divmod(index, BAND)
    return (ka // 2) * 2 + (band // 4) % 2, ka % 2, band // MEMBERS, band % 4


def index_of(x, core, y, z):
    x, core, y, z = x % 4, core % 2, y % 4, z % 4
    return ((x // 2) * 2 + core) * BAND + y * MEMBERS + (x % 2) * 4 + z


def shifted(value, x=0, core=0, y=0, z=0):
    pairs = []
    for index in range(KA * BAND):
        px, pc, py, pz = place(index)
        pairs.append((index, index_of(px + x, pc + core, py + y, pz + z)))
    return lax.ppermute(value, ("ka", "band"), pairs)


def from_next(value, y):
    pairs = []
    for index in range(KA * BAND):
        ka, band = divmod(index, BAND)
        source = ((ka + 1) % KA) * BAND + (band + y * MEMBERS) % BAND
        pairs.append((source, index))
    return lax.ppermute(value, ("ka", "band"), pairs)


def local(occ_orb, occ_energy, emp_orb, emp_energy, gidx, sym_map, weights, count):
    ka = lax.axis_index("ka")
    band = lax.axis_index("band")
    core = ka % 2
    y = band // MEMBERS
    member = band % MEMBERS
    x = (ka // 2) * 2 + member // 4
    z = member % 4

    energy = jnp.broadcast_to(emp_energy[:, :, None, None], (KLOC, 2, 8, 128))
    lines = jnp.concatenate([emp_orb.reshape(KLOC, 2, 2 * LINES, 128), energy], axis=2)
    here = [lines[1]] + [shifted(lines[1], y=-step) for step in range(1, YS)]
    after = [from_next(lines[0], step) for step in range(YS)]
    emp = jnp.concatenate(here + after, axis=0)
    occ = jnp.transpose(occ_orb, (0, 2, 1, 3))

    kpoint = ka * KLOC + jnp.arange(KLOC, dtype=jnp.int32)
    wrapped = (kpoint + 1 >= KA * KLOC).astype(jnp.int32)
    target = kpoint + 1 - wrapped * (KA * KLOC)
    odd = (gidx // GRID) % 2
    outer = (gidx // (2 * GRID)) % 8
    places = (gidx // PLANE * PLANE + odd * HALF + outer * GRID + gidx % GRID) * 8

    wsum = jnp.sum(weights).astype(jnp.float32)
    scale = -4.0 / jnp.sqrt(jnp.float32(VB * 2 * BAND) * wsum) / POINTS
    owner = (y + jnp.arange(YS, dtype=jnp.int32)) % YS
    bands = owner[:, None] * (2 * MEMBERS) + member * 2 + jnp.arange(2, dtype=jnp.int32)[None, :]
    live = (bands[None] < count[target][:, None, None]).astype(jnp.float32)
    gap = emp[:, 2 * LINES, 0].reshape(KLOC, YS, 2)[..., None] - occ_energy[:, None, None, :]
    strength = (scale * weights[kpoint].astype(jnp.float32))[:, None, None, None]
    factor = (strength * live[..., None] / gap).reshape(KLOC * YS, CHUNK)

    near_core = jnp.arange(2, dtype=jnp.int32)[:, None, None]
    to_x = (x + jnp.arange(4, dtype=jnp.int32)[None, :, None]) % 4
    to_z = (z + jnp.arange(4, dtype=jnp.int32)[None, None, :]) % 4
    to_ka = (to_x // 2) * 2 + (core + near_core) % 2
    rows = (to_ka * 256 + y * 64 + (to_x % 2) * 32 + to_z * 8).reshape(32)
    rows = jnp.concatenate([rows, wrapped * (PLANE * 8)])

    near, far = partial_rows(places, sym_map, rows.astype(jnp.int32), occ, emp, factor)

    both = near + shifted(far, core=1)
    both = both.reshape(2, 4, 4, 8, NG)
    first = both[..., : NG // 2]
    second = both[..., NG // 2 :]
    first_parts = [shifted(first[:, :, step], z=step) for step in range(1, 4)]
    second_parts = [shifted(second[:, step], x=step) for step in range(1, 4)]
    first = first[:, :, 0] + (first_parts[0] + first_parts[1]) + first_parts[2]
    second = second[:, 0] + (second_parts[0] + second_parts[1]) + second_parts[2]
    first_parts = [shifted(first[:, step], x=step) for step in range(1, 4)]
    second_parts = [shifted(second[:, step], z=step) for step in range(1, 4)]
    first = first[:, 0] + (first_parts[0] + first_parts[1]) + first_parts[2]
    second = second[:, 0] + (second_parts[0] + second_parts[1]) + second_parts[2]
    owned = jnp.concatenate([first, second], axis=2)
    return jnp.transpose(owned, (1, 0, 2))[None]


def solution(mesh):
    return jax.shard_map(
        local,
        mesh=mesh,
        in_specs=(
            P("ka", None, None, None),
            P("ka", None),
            P("ka", "band", None, None),
            P("ka", "band"),
            P(),
            P("ka", None),
            P(),
            P(),
        ),
        out_specs=P(None, ("ka", "band"), None, None),
        check_vma=False,
    )
```

```python
import functools

import jax
import jax.numpy as jnp
import numpy as np
from jax import lax
from jax.experimental import pallas as pl
from jax.experimental.pallas import tpu as pltpu
from jax.sharding import Mesh, PartitionSpec as P

GRID = 16
PLANE = GRID * GRID
POINTS = GRID * PLANE
HALF = PLANE // 2
NG = 2048
VB = 64
KA_AXES = ("x_hi", "core")
BAND_AXES = ("y", "x_lo", "z")
KA = 4
BAND = 32
YS = 4
MEMBERS = BAND // YS
CHUNK = 2 * VB
KLOC = 2
DEPTH = KLOC * YS * 2 * CHUNK
ROWS = 256
OWNERS = ROWS // 16
LINES = POINTS // 128


def plane_matrices():
    point = np.arange(HALF)
    outer, inner = point // GRID, point % GRID
    parts = []
    for parity in range(2):
        turns = np.outer(2 * outer + parity, outer) + np.outer(inner, inner)
        angle = 2.0 * np.pi * (turns % GRID) / GRID
        cos, sin = np.cos(angle), np.sin(angle)
        parts.append(np.block([[cos, sin], [-sin, cos]]))
    whole = np.stack(parts).astype(np.float32)
    high = whole.astype(jnp.bfloat16)
    low = (whole - high.astype(np.float32)).astype(jnp.bfloat16)
    return high, low


def split(value):
    high = value.astype(jnp.bfloat16)
    low = (value - high.astype(jnp.float32)).astype(jnp.bfloat16)
    return high, low


def four(points):
    (ar, ai), (br, bi), (cr, ci), (dr, di) = points
    sr, si = ar + cr, ai + ci
    tr, ti = ar - cr, ai - ci
    ur, ui = br + dr, bi + di
    wr, wi = br - dr, bi - di
    return [(sr + ur, si + ui), (tr + wi, ti - wr), (sr - ur, si - ui), (tr - wi, ti + wr)]


def turned(point, power):
    re, im = point
    power %= GRID
    if power == 0:
        return re, im
    if power == 4:
        return im, -re
    if power == 2:
        root = float(np.sqrt(0.5))
        return (re + im) * root, (im - re) * root
    if power == 6:
        root = float(np.sqrt(0.5))
        return (im - re) * root, (re + im) * -root
    cos = float(np.cos(2 * np.pi * power / GRID))
    sin = float(np.sin(2 * np.pi * power / GRID))
    return re * cos + im * sin, im * cos - re * sin


def dot_t(left, right):
    return lax.dot_general(left, right, (((1,), (1,)), ((), ())), preferred_element_type=jnp.float32)


def kernel(
    place_ref, sym_ref, rows_ref, occ_hbm, emp_ref, fac_ref, whi_ref, wlo_ref, near_ref, far_ref,
    occ_ref, mid_ref, xhi0_ref, xlo0_ref, xhi1_ref, xlo1_ref, spec_ref, left_ref,
    pick0_ref, pick1_ref, pick2_ref, pick3_ref, bhi_ref, blo_ref, ahi_ref, alo_ref, idx_ref, sems,
):
    slots = ((xhi0_ref, xlo0_ref), (xhi1_ref, xlo1_ref))
    picks = (pick0_ref, pick1_ref, pick2_ref, pick3_ref)
    copies = [
        [pltpu.make_async_copy(occ_hbm.at[k, :, part], occ_ref.at[k, part], sems.at[k, part]) for part in range(2)]
        for k in range(KLOC)
    ]
    for copy in copies[0] + copies[1]:
        copy.start()

    def pairs(step, block, slot):
        xhi_ref, xlo_ref = slots[slot]
        k = step // YS
        band = block // (VB // 16)
        start = pl.multiple_of((block % (VB // 16)) * 16, 16)
        line = step * 2 + band

        def pair(a, half):
            base = a * PLANE + half * HALF
            o_re = occ_ref[k, 0, pl.ds(start, 16), pl.ds(base, HALF)]
            o_im = occ_ref[k, 1, pl.ds(start, 16), pl.ds(base, HALF)]
            at = a * 2 + half
            e_re = emp_ref[line, at : at + 1, :]
            e_im = emp_ref[line, LINES + at : LINES + at + 1, :]
            return o_re * e_re + o_im * e_im, o_re * e_im - o_im * e_re

        for a0 in range(4):
            even, odd = [], []
            for a1 in range(4):
                fr, fi = pair(4 * a1 + a0, 0)
                sr, si = pair(4 * a1 + a0, 1)
                even.append((fr + sr, fi + si))
                odd.append((fr - sr, fi - si))
            for parity, points in enumerate((even, odd)):
                for k0, point in enumerate(four(points)):
                    re, im = turned(point, a0 * k0)
                    mid_ref[parity, k0, a0, 0] = re
                    mid_ref[parity, k0, a0, 1] = im
        row = pl.multiple_of(block * 16, 16)
        for parity in range(2):
            for k0 in range(4):
                points = [(mid_ref[parity, k0, a0, 0], mid_ref[parity, k0, a0, 1]) for a0 in range(4)]
                for k1, point in enumerate(four(points)):
                    at = k0 + 4 * k1
                    for part in range(2):
                        high, low = split(point[part])
                        xhi_ref[parity, pl.ds(at * CHUNK + row, 16), pl.ds(part * HALF, HALF)] = high
                        xlo_ref[parity, pl.ds(at * CHUNK + row, 16), pl.ds(part * HALF, HALF)] = low

    def places(step, block):
        base = (step * 8 + block) * 64
        shift = rows_ref[ROWS // 8 + step // YS]
        for lane in range(64):
            idx_ref[base + lane] = (place_ref[sym_ref[base + lane]] + shift) & (POINTS * 8 - 1)

    def planes(step, tile, slot):
        xhi_ref, xlo_ref = slots[slot]
        chunk = step % YS
        for parity in range(2):
            at = pl.ds(pl.multiple_of(tile * 2 * CHUNK, 2 * CHUNK), 2 * CHUNK)
            xhi = xhi_ref[parity, at, :]
            xlo = xlo_ref[parity, at, :]
            whi = whi_ref[parity]
            wide = dot_t(jnp.concatenate([whi, wlo_ref[parity]], axis=0), xhi)
            out = dot_t(whi, xlo) + wide[:PLANE] + wide[PLANE:]
            for which in range(2):
                base = ((tile * 2 + which) * PLANE + parity * HALF) * 8 + chunk * 2
                for part in range(2):
                    spec_ref[pl.ds(base + part, HALF, stride=8), :] = out[
                        part * HALF : (part + 1) * HALF, which * CHUNK : (which + 1) * CHUNK
                    ]

    def columns(k, slot):
        return pl.ds(pl.multiple_of(k * (8 * CHUNK) + slot * CHUNK, CHUNK), CHUNK)

    def gather(k):
        def pick(at, to_ref, to):
            source = pl.multiple_of(idx_ref[k * NG + at], 8)
            to_ref[pl.ds(to, 8), :] = spec_ref[pl.ds(source, 8), :]

        def left(step, carry):
            row = pl.multiple_of(step * 16, 16)
            for lane in range(16):
                pick(rows_ref[step * 2 + lane // 8] + lane % 8, left_ref, lane * 8)
            for chunk in range(YS):
                factor = fac_ref[pl.ds(k * YS + chunk, 1), :]
                re = left_ref[pl.ds(2 * chunk, 16, stride=8), :] * factor
                im = left_ref[pl.ds(2 * chunk + 1, 16, stride=8), :] * factor
                rhi, rlo = split(re)
                ihi, ilo = split(im)
                first, second = columns(k, 2 * chunk), columns(k, 2 * chunk + 1)
                ahi_ref[pl.ds(row, 16), first] = rhi
                alo_ref[pl.ds(row, 16), first] = rlo
                ahi_ref[pl.ds(row, 16), second] = ihi
                alo_ref[pl.ds(row, 16), second] = ilo
                ahi_ref[pl.ds(ROWS + row, 16), first] = -ihi
                alo_ref[pl.ds(ROWS + row, 16), first] = -ilo
                ahi_ref[pl.ds(ROWS + row, 16), second] = rhi
                alo_ref[pl.ds(ROWS + row, 16), second] = rlo
            return carry

        lax.fori_loop(0, ROWS // 16, left, 0)

        def right(step, carry):
            for which, pick_ref in enumerate(picks):
                row = pl.multiple_of(step * (16 * len(picks)) + which * 16, 16)
                for lane in range(16):
                    pick(row + lane, pick_ref, lane * 8)
                for slot in range(8):
                    high, low = split(pick_ref[pl.ds(slot, 16, stride=8), :])
                    bhi_ref[pl.ds(row, 16), columns(k, slot)] = high
                    blo_ref[pl.ds(row, 16), columns(k, slot)] = low
            return carry

        lax.fori_loop(0, NG // (16 * len(picks)), right, 0)

    def first(block, carry):
        pairs(0, block, 0)
        places(0, block)
        return carry

    def both(step, slot):
        def body(turn, carry):
            for part in range(2):
                planes(step - 1, turn * 2 + part, 1 - slot)
                pairs(step, turn * 2 + part, slot)
                places(step, turn * 2 + part)
            return carry

        lax.fori_loop(0, 4, body, 0)

    def last(block, carry):
        for part in range(4):
            planes(KLOC * YS - 1, block * 4 + part, 1)
        return carry

    for copy in copies[0]:
        copy.wait()
    lax.fori_loop(0, 8, first, 0)

    def two(turn, carry):
        both(2 * turn + 1, 1)

        @pl.when(turn == 1)
        def _():
            for copy in copies[1]:
                copy.wait()

        both(2 * turn + 2, 0)

        @pl.when(turn == 1)
        def _():
            gather(0)

        return carry

    lax.fori_loop(0, 3, two, 0)
    both(KLOC * YS - 1, 1)
    lax.fori_loop(0, 2, last, 0)
    gather(1)

    def one_column(tile, carry):
        at = pl.ds(pl.multiple_of(tile * 256, 256), 256)
        bhi = bhi_ref[at, :]
        blo = blo_ref[at, :]
        ahi = ahi_ref[...]
        out = dot_t(ahi, bhi) + dot_t(ahi, blo) + dot_t(alo_ref[...], bhi)
        for part in range(2):
            for to in range(OWNERS):
                row = part * ROWS + to * 8
                near_ref[to, part, :, at] = out[row : row + 8]
                far_ref[to, part, :, at] = out[row + ROWS // 2 : row + ROWS // 2 + 8]
        return carry

    lax.fori_loop(0, NG // 256, one_column, 0)


def partial_rows(places, sym_map, rows, occ, emp, factor):
    whi, wlo = plane_matrices()
    vmem = pl.BlockSpec(memory_space=pltpu.VMEM)
    smem = pl.BlockSpec(memory_space=pltpu.SMEM)
    part = jax.ShapeDtypeStruct((OWNERS, 2, 8, NG), jnp.float32)
    return pl.pallas_call(
        kernel,
        out_shape=(part, part),
        in_specs=[smem, smem, smem, pl.BlockSpec(memory_space=pl.ANY), vmem, vmem, vmem, vmem],
        out_specs=(vmem, vmem),
        scratch_shapes=[
            pltpu.VMEM((KLOC, 2, VB, POINTS), jnp.float32),
            pltpu.VMEM((2, 4, 4, 2, 16, HALF), jnp.float32),
            pltpu.VMEM((2, GRID * CHUNK, PLANE), jnp.bfloat16),
            pltpu.VMEM((2, GRID * CHUNK, PLANE), jnp.bfloat16),
            pltpu.VMEM((2, GRID * CHUNK, PLANE), jnp.bfloat16),
            pltpu.VMEM((2, GRID * CHUNK, PLANE), jnp.bfloat16),
            pltpu.VMEM((POINTS * 8, CHUNK), jnp.float32),
            pltpu.VMEM((16 * 8, CHUNK), jnp.float32),
            pltpu.VMEM((16 * 8, CHUNK), jnp.float32),
            pltpu.VMEM((16 * 8, CHUNK), jnp.float32),
            pltpu.VMEM((16 * 8, CHUNK), jnp.float32),
            pltpu.VMEM((16 * 8, CHUNK), jnp.float32),
            pltpu.VMEM((NG, DEPTH), jnp.bfloat16),
            pltpu.VMEM((NG, DEPTH), jnp.bfloat16),
            pltpu.VMEM((2 * ROWS, DEPTH), jnp.bfloat16),
            pltpu.VMEM((2 * ROWS, DEPTH), jnp.bfloat16),
            pltpu.SMEM((KLOC * NG,), jnp.int32),
            pltpu.SemaphoreType.DMA((KLOC, 2)),
        ],
        compiler_params=pltpu.CompilerParams(vmem_limit_bytes=62 * 2**20),
        cost_estimate=pl.CostEstimate(flops=40 * 10**9, bytes_accessed=10 * 2**20, transcendentals=0),
    )(places, sym_map, rows, occ, emp, factor, jnp.asarray(whi), jnp.asarray(wlo))


def shifted(value, axis, by):
    size = lax.axis_size(axis)
    return lax.ppermute(value, axis, [(index, (index + by) % size) for index in range(size)])


def local(occ_orb, occ_energy, emp_orb, emp_energy, gidx, sym_map, weights, count):
    ka = lax.axis_index(KA_AXES)
    core = lax.axis_index("core")
    y = lax.axis_index("y")
    member = lax.axis_index(("x_lo", "z"))

    energy = jnp.broadcast_to(emp_energy[:, :, None, None], (KLOC, 2, 8, 128))
    lines = jnp.concatenate([emp_orb.reshape(KLOC, 2, 2 * LINES, 128), energy], axis=2)
    own = jnp.stack([lines[1], shifted(lines[0], KA_AXES, -1)])
    emp = jnp.concatenate([own] + [shifted(own, "y", -step) for step in range(1, YS)], axis=1)
    emp = emp.reshape(KLOC * YS * 2, 2 * LINES + 8, 128)

    kpoint = ka * KLOC + jnp.arange(KLOC, dtype=jnp.int32)
    wrapped = (kpoint + 1 >= KA * KLOC).astype(jnp.int32)
    target = kpoint + 1 - wrapped * (KA * KLOC)
    odd = (gidx // GRID) % 2
    outer = (gidx // (2 * GRID)) % 8
    places = (gidx // PLANE * PLANE + odd * HALF + outer * GRID + gidx % GRID) * 8

    wsum = jnp.sum(weights).astype(jnp.float32)
    scale = -4.0 / jnp.sqrt(jnp.float32(VB * 2 * BAND) * wsum) / POINTS
    owner = (y + jnp.arange(YS, dtype=jnp.int32)) % YS
    bands = owner[:, None] * (2 * MEMBERS) + member * 2 + jnp.arange(2, dtype=jnp.int32)[None, :]
    live = (bands[None] < count[target][:, None, None]).astype(jnp.float32)
    gap = emp[:, 2 * LINES, 0].reshape(KLOC, YS, 2)[..., None] - occ_energy[:, None, None, :]
    strength = (scale * weights[kpoint].astype(jnp.float32))[:, None, None, None]
    factor = (strength * live[..., None] / gap).reshape(KLOC * YS, CHUNK)

    near_core = jnp.arange(2, dtype=jnp.int32)[:, None, None]
    x = lax.axis_index(("x_hi", "x_lo"))
    z = lax.axis_index("z")
    to_x = (x + jnp.arange(4, dtype=jnp.int32)[None, :, None]) % 4
    to_z = (z + jnp.arange(4, dtype=jnp.int32)[None, None, :]) % 4
    to_ka = (to_x // 2) * 2 + (core + near_core) % 2
    rows = (to_ka * 256 + y * 64 + (to_x % 2) * 32 + to_z * 8).reshape(32)
    rows = jnp.concatenate([rows, wrapped * (PLANE * 8)])

    near, far = partial_rows(places, sym_map.reshape(KLOC * NG), rows.astype(jnp.int32), occ_orb, emp, factor)

    both = near + shifted(far, "core", 1)
    both = both.reshape(4, 4, 2, 8, NG)
    x_axes = ("x_hi", "x_lo")

    def added(own, parts):
        return own + (parts[0] + parts[1]) + parts[2]

    first, second = both[:, :, 0], both[:, :, 1]
    first_parts = [shifted(first[:, step], "z", step) for step in range(1, 4)]
    second_parts = [shifted(second[step], x_axes, step) for step in range(1, 4)]
    first = added(first[:, 0], first_parts)
    second = added(second[0], second_parts)
    first_parts = [shifted(first[step], x_axes, step) for step in range(1, 4)]
    second_parts = [shifted(second[step], "z", step) for step in range(1, 4)]
    owned = jnp.stack([added(first[0], first_parts), added(second[0], second_parts)], axis=1)
    return owned[None]


def solution(mesh):
    fine = Mesh(mesh.devices.reshape(2, 2, YS, 2, 4), KA_AXES + BAND_AXES)
    return jax.shard_map(
        local,
        mesh=fine,
        in_specs=(
            P(KA_AXES, None, None, None),
            P(KA_AXES, None),
            P(KA_AXES, BAND_AXES, None, None),
            P(KA_AXES, BAND_AXES),
            P(),
            P(KA_AXES, None),
            P(),
            P(),
        ),
        out_specs=P(None, KA_AXES + BAND_AXES, None, None),
        check_vma=False,
    )
```

```python
import functools

import jax
import jax.numpy as jnp
import numpy as np
from jax import lax
from jax.experimental import pallas as pl
from jax.experimental.pallas import tpu as pltpu
from jax.sharding import Mesh, PartitionSpec as P

GRID = 16
PLANE = GRID * GRID
POINTS = GRID * PLANE
HALF = PLANE // 2
NG = 2048
VB = 64
KA_AXES = ("x_hi", "core")
BAND_AXES = ("y", "x_lo", "z")
KA = 4
BAND = 32
YS = 4
MEMBERS = BAND // YS
CHUNK = 2 * VB
KLOC = 2
DEPTH = YS * 2 * CHUNK
ROWS = 256
OWNERS = ROWS // 16
WIDE = POINTS + 128


def plane_matrices():
    point = np.arange(HALF)
    outer, inner = point // GRID, point % GRID
    parts = []
    for parity in range(2):
        turns = np.outer(2 * outer + parity, outer) + np.outer(inner, inner)
        angle = 2.0 * np.pi * (turns % GRID) / GRID
        cos, sin = np.cos(angle), np.sin(angle)
        parts.append(np.block([[cos, sin], [-sin, cos]]))
    whole = np.stack(parts).astype(np.float32)
    high = whole.astype(jnp.bfloat16)
    low = (whole - high.astype(np.float32)).astype(jnp.bfloat16)
    return high, low


def split(value):
    high = value.astype(jnp.bfloat16)
    low = (value - high.astype(jnp.float32)).astype(jnp.bfloat16)
    return high, low


def four(points):
    (ar, ai), (br, bi), (cr, ci), (dr, di) = points
    sr, si = ar + cr, ai + ci
    tr, ti = ar - cr, ai - ci
    ur, ui = br + dr, bi + di
    wr, wi = br - dr, bi - di
    return [(sr + ur, si + ui), (tr + wi, ti - wr), (sr - ur, si - ui), (tr - wi, ti + wr)]


def turned(point, power):
    re, im = point
    power %= GRID
    if power == 0:
        return re, im
    if power == 4:
        return im, -re
    if power == 2:
        root = float(np.sqrt(0.5))
        return (re + im) * root, (im - re) * root
    if power == 6:
        root = float(np.sqrt(0.5))
        return (im - re) * root, (re + im) * -root
    cos = float(np.cos(2 * np.pi * power / GRID))
    sin = float(np.sin(2 * np.pi * power / GRID))
    return re * cos + im * sin, im * cos - re * sin


def dot_t(left, right):
    return lax.dot_general(left, right, (((1,), (1,)), ((), ())), preferred_element_type=jnp.float32)


def kernel(
    place_ref, sym_ref, rows_ref, occ_hbm, emp_hbm, fac_ref, whi_hbm, wlo_hbm, near_hbm, far_hbm,
    occ_ref, emp_ref, whi_ref, wlo_ref, mid_ref, xhi0_ref, xlo0_ref, xhi1_ref, xlo1_ref, spec_ref, left_ref,
    pick0_ref, pick1_ref, pick2_ref, pick3_ref, bhi0_ref, blo0_ref, bhi1_ref, blo1_ref,
    ahi0_ref, alo0_ref, ahi1_ref, alo1_ref, near_ref, far_ref, idx_ref, occ_sems, in_sems, out_sems,
):
    slots = ((xhi0_ref, xlo0_ref), (xhi1_ref, xlo1_ref))
    picks = (pick0_ref, pick1_ref, pick2_ref, pick3_ref)
    rights = ((bhi0_ref, blo0_ref), (bhi1_ref, blo1_ref))
    lefts = ((ahi0_ref, alo0_ref), (ahi1_ref, alo1_ref))
    copies = [
        [pltpu.make_async_copy(occ_hbm.at[k, :, part], occ_ref.at[k, part], occ_sems.at[k, part]) for part in range(2)]
        for k in range(KLOC)
    ]
    others = [
        pltpu.make_async_copy(source, target, in_sems.at[which])
        for which, (source, target) in enumerate(((emp_hbm, emp_ref), (whi_hbm, whi_ref), (wlo_hbm, wlo_ref)))
    ]
    for copy in [others[0]] + copies[0] + others[1:] + copies[1]:
        copy.start()

    def pairs(step, block, slot):
        xhi_ref, xlo_ref = slots[slot]
        k = step // YS
        band = block // (VB // 16)
        start = pl.multiple_of((block % (VB // 16)) * 16, 16)
        line = step * 2 + band

        def pair(a, half):
            base = a * PLANE + half * HALF
            o_re = occ_ref[k, 0, pl.ds(start, 16), pl.ds(base, HALF)]
            o_im = occ_ref[k, 1, pl.ds(start, 16), pl.ds(base, HALF)]
            e_re = emp_ref[line, 0:1, pl.ds(base, HALF)]
            e_im = emp_ref[line, 1:2, pl.ds(base, HALF)]
            return o_re * e_re + o_im * e_im, o_re * e_im - o_im * e_re

        for a0 in range(4):
            even, odd = [], []
            for a1 in range(4):
                fr, fi = pair(4 * a1 + a0, 0)
                sr, si = pair(4 * a1 + a0, 1)
                even.append((fr + sr, fi + si))
                odd.append((fr - sr, fi - si))
            for parity, points in enumerate((even, odd)):
                for k0, point in enumerate(four(points)):
                    re, im = turned(point, a0 * k0)
                    mid_ref[parity, k0, a0, 0] = re
                    mid_ref[parity, k0, a0, 1] = im
        row = pl.multiple_of(block * 16, 16)
        for parity in range(2):
            for k0 in range(4):
                points = [(mid_ref[parity, k0, a0, 0], mid_ref[parity, k0, a0, 1]) for a0 in range(4)]
                for k1, point in enumerate(four(points)):
                    at = k0 + 4 * k1
                    for part in range(2):
                        high, low = split(point[part])
                        xhi_ref[parity, pl.ds(at * CHUNK + row, 16), pl.ds(part * HALF, HALF)] = high
                        xlo_ref[parity, pl.ds(at * CHUNK + row, 16), pl.ds(part * HALF, HALF)] = low

    def places(step, block):
        base = (step * 8 + block) * 64
        shift = rows_ref[ROWS // 8 + step // YS]
        for lane in range(64):
            idx_ref[base + lane] = (place_ref[sym_ref[base + lane]] + shift) & (POINTS * 8 - 1)

    def planes(step, tile, slot):
        xhi_ref, xlo_ref = slots[slot]
        chunk = step % YS
        for parity in range(2):
            at = pl.ds(pl.multiple_of(tile * 2 * CHUNK, 2 * CHUNK), 2 * CHUNK)
            xhi = xhi_ref[parity, at, :]
            xlo = xlo_ref[parity, at, :]
            whi = whi_ref[parity]
            wide = dot_t(jnp.concatenate([whi, wlo_ref[parity]], axis=0), xhi)
            out = dot_t(whi, xlo) + wide[:PLANE] + wide[PLANE:]
            for which in range(2):
                base = ((tile * 2 + which) * PLANE + parity * HALF) * 8 + chunk * 2
                for part in range(2):
                    spec_ref[pl.ds(base + part, HALF, stride=8), :] = out[
                        part * HALF : (part + 1) * HALF, which * CHUNK : (which + 1) * CHUNK
                    ]

    def columns(slot):
        return pl.ds(slot * CHUNK, CHUNK)

    def pick(k, at, to_ref, to):
        source = pl.multiple_of(idx_ref[k * NG + at], 8)
        to_ref[pl.ds(to, 8), :] = spec_ref[pl.ds(source, 8), :]

    def gather_left(k):
        ahi_ref, alo_ref = lefts[k]

        def left(step, carry):
            row = pl.multiple_of(step * 16, 16)
            for lane in range(16):
                pick(k, rows_ref[step * 2 + lane // 8] + lane % 8, left_ref, lane * 8)
            for chunk in range(YS):
                factor = fac_ref[k * YS + chunk : k * YS + chunk + 1, :]
                re = left_ref[pl.ds(2 * chunk, 16, stride=8), :] * factor
                im = left_ref[pl.ds(2 * chunk + 1, 16, stride=8), :] * factor
                rhi, rlo = split(re)
                ihi, ilo = split(im)
                first, second = columns(2 * chunk), columns(2 * chunk + 1)
                ahi_ref[pl.ds(row, 16), first] = rhi
                alo_ref[pl.ds(row, 16), first] = rlo
                ahi_ref[pl.ds(row, 16), second] = ihi
                alo_ref[pl.ds(row, 16), second] = ilo
                ahi_ref[pl.ds(ROWS + row, 16), first] = -ihi
                alo_ref[pl.ds(ROWS + row, 16), first] = -ilo
                ahi_ref[pl.ds(ROWS + row, 16), second] = rhi
                alo_ref[pl.ds(ROWS + row, 16), second] = rlo
            return carry

        lax.fori_loop(0, ROWS // 16, left, 0)

    def gather(k):
        bhi_ref, blo_ref = rights[k]
        gather_left(k)

        def right(step, carry):
            for which, pick_ref in enumerate(picks):
                row = pl.multiple_of(step * (16 * len(picks)) + which * 16, 16)
                for lane in range(16):
                    pick(k, row + lane, pick_ref, lane * 8)
                for slot in range(8):
                    high, low = split(pick_ref[pl.ds(slot, 16, stride=8), :])
                    bhi_ref[pl.ds(row, 16), columns(slot)] = high
                    blo_ref[pl.ds(row, 16), columns(slot)] = low
            return carry

        lax.fori_loop(0, NG // (16 * len(picks)), right, 0)

    def product(k, at):
        (ahi_ref, alo_ref), (bhi_ref, blo_ref) = lefts[k], rights[k]
        bhi = bhi_ref[at, :]
        ahi = ahi_ref[...]
        return dot_t(ahi, bhi) + dot_t(ahi, blo_ref[at, :]) + dot_t(alo_ref[...], bhi)

    def first(block, carry):
        pairs(0, block, 0)
        places(0, block)
        return carry

    def both(step, slot):
        def body(turn, carry):
            for part in range(2):
                planes(step - 1, turn * 2 + part, 1 - slot)
                pairs(step, turn * 2 + part, slot)
                places(step, turn * 2 + part)
            return carry

        lax.fori_loop(0, 4, body, 0)

    def last(block, carry):
        for part in range(4):
            planes(KLOC * YS - 1, block * 4 + part, 1)
        return carry

    for copy in copies[0] + others:
        copy.wait()
    lax.fori_loop(0, 8, first, 0)

    def two(turn, carry):
        both(2 * turn + 1, 1)

        @pl.when(turn == 1)
        def _():
            for copy in copies[1]:
                copy.wait()

        both(2 * turn + 2, 0)

        @pl.when(turn == 1)
        def _():
            gather(0)

        return carry

    lax.fori_loop(0, 3, two, 0)
    both(KLOC * YS - 1, 1)
    lax.fori_loop(0, 2, last, 0)
    gather(1)

    def places_of(tile):
        return pl.ds(pl.multiple_of(tile * 256, 256), 256)

    def sent(tile):
        return [
            pltpu.make_async_copy(
                source.at[:, :, :, places_of(tile)], target.at[:, :, :, places_of(tile)], out_sems.at[tile, which]
            )
            for which, (source, target) in enumerate(((near_ref, near_hbm), (far_ref, far_hbm)))
        ]

    def one_column(tile, carry):
        out = product(0, places_of(tile)) + product(1, places_of(tile))
        for part in range(2):
            for to in range(OWNERS):
                row = part * ROWS + to * 8
                near_ref[to, part, :, places_of(tile)] = out[row : row + 8]
                far_ref[to, part, :, places_of(tile)] = out[row + ROWS // 2 : row + ROWS // 2 + 8]
        for copy in sent(tile):
            copy.start()
        return carry

    def done(tile, carry):
        for copy in sent(tile):
            copy.wait()
        return carry

    lax.fori_loop(0, NG // 256, one_column, 0)
    lax.fori_loop(0, NG // 256, done, 0)


def partial_rows(places, sym_map, rows, occ, emp, factor):
    whi, wlo = plane_matrices()
    vmem = pl.BlockSpec(memory_space=pltpu.VMEM)
    smem = pl.BlockSpec(memory_space=pltpu.SMEM)
    hbm = pl.BlockSpec(memory_space=pl.ANY)
    part = jax.ShapeDtypeStruct((OWNERS, 2, 8, NG), jnp.float32)
    return pl.pallas_call(
        kernel,
        out_shape=(part, part),
        in_specs=[smem, smem, smem, hbm, hbm, vmem, hbm, hbm],
        out_specs=(hbm, hbm),
        scratch_shapes=[
            pltpu.VMEM((KLOC, 2, VB, POINTS), jnp.float32),
            pltpu.VMEM((KLOC * YS * 2, 2, WIDE), jnp.float32),
            pltpu.VMEM((2, PLANE, PLANE), jnp.bfloat16),
            pltpu.VMEM((2, PLANE, PLANE), jnp.bfloat16),
            pltpu.VMEM((2, 4, 4, 2, 16, HALF), jnp.float32),
        ]
        + [pltpu.VMEM((2, GRID * CHUNK, PLANE), jnp.bfloat16)] * 4
        + [pltpu.VMEM((POINTS * 8, CHUNK), jnp.float32)]
        + [pltpu.VMEM((16 * 8, CHUNK), jnp.float32)] * 5
        + [pltpu.VMEM((NG, DEPTH), jnp.bfloat16)] * 4
        + [pltpu.VMEM((2 * ROWS, DEPTH), jnp.bfloat16)] * 4
        + [pltpu.VMEM((OWNERS, 2, 8, NG), jnp.float32)] * 2
        + [
            pltpu.SMEM((KLOC * NG,), jnp.int32),
            pltpu.SemaphoreType.DMA((KLOC, 2)),
            pltpu.SemaphoreType.DMA((3,)),
            pltpu.SemaphoreType.DMA((NG // 256, 2)),
        ],
        compiler_params=pltpu.CompilerParams(vmem_limit_bytes=62 * 2**20),
        cost_estimate=pl.CostEstimate(flops=40 * 10**9, bytes_accessed=10 * 2**20, transcendentals=0),
    )(places, sym_map, rows, occ, emp, factor, jnp.asarray(whi), jnp.asarray(wlo))


def shifted(value, axis, by):
    size = lax.axis_size(axis)
    return lax.ppermute(value, axis, [(index, (index + by) % size) for index in range(size)])


def local(occ_orb, occ_energy, emp_orb, emp_energy, gidx, sym_map, weights, count):
    ka = lax.axis_index(KA_AXES)
    core = lax.axis_index("core")
    y = lax.axis_index("y")
    member = lax.axis_index(("x_lo", "z"))

    energy = jnp.broadcast_to(emp_energy[:, :, None, None], (KLOC, 2, 2, 128))
    lines = jnp.concatenate([emp_orb, energy], axis=3)
    own = jnp.stack([lines[1], shifted(lines[0], KA_AXES, -1)])
    emp = jnp.concatenate([own] + [shifted(own, "y", -step) for step in range(1, YS)], axis=1)
    emp = emp.reshape(KLOC * YS * 2, 2, WIDE)

    kpoint = ka * KLOC + jnp.arange(KLOC, dtype=jnp.int32)
    wrapped = (kpoint + 1 >= KA * KLOC).astype(jnp.int32)
    target = kpoint + 1 - wrapped * (KA * KLOC)
    odd = (gidx // GRID) % 2
    outer = (gidx // (2 * GRID)) % 8
    places = (gidx // PLANE * PLANE + odd * HALF + outer * GRID + gidx % GRID) * 8

    wsum = jnp.sum(weights).astype(jnp.float32)
    scale = -4.0 / jnp.sqrt(jnp.float32(VB * 2 * BAND) * wsum) / POINTS
    owner = (y + jnp.arange(YS, dtype=jnp.int32)) % YS
    bands = owner[:, None] * (2 * MEMBERS) + member * 2 + jnp.arange(2, dtype=jnp.int32)[None, :]
    live = (bands[None] < count[target][:, None, None]).astype(jnp.float32)
    gap = emp[:, 0, POINTS].reshape(KLOC, YS, 2)[..., None] - occ_energy[:, None, None, :]
    strength = (scale * weights[kpoint].astype(jnp.float32))[:, None, None, None]
    factor = (strength * live[..., None] / gap).reshape(KLOC * YS, CHUNK)

    near_core = jnp.arange(2, dtype=jnp.int32)[:, None, None]
    x = lax.axis_index(("x_hi", "x_lo"))
    z = lax.axis_index("z")
    to_x = (x + jnp.arange(4, dtype=jnp.int32)[None, :, None]) % 4
    to_z = (z + jnp.arange(4, dtype=jnp.int32)[None, None, :]) % 4
    to_ka = (to_x // 2) * 2 + (core + near_core) % 2
    rows = (to_ka * 256 + y * 64 + (to_x % 2) * 32 + to_z * 8).reshape(32)
    rows = jnp.concatenate([rows, wrapped * (PLANE * 8)])

    near, far = partial_rows(places, sym_map.reshape(KLOC * NG), rows.astype(jnp.int32), occ_orb, emp, factor)

    both = near + shifted(far, "core", 1)
    both = both.reshape(4, 4, 2, 8, NG)
    x_axes = ("x_hi", "x_lo")

    def added(own, parts):
        return own + (parts[0] + parts[1]) + parts[2]

    first, second = both[:, :, 0], both[:, :, 1]
    first_parts = [shifted(first[:, step], "z", step) for step in range(1, 4)]
    second_parts = [shifted(second[step], x_axes, step) for step in range(1, 4)]
    first = added(first[:, 0], first_parts)
    second = added(second[0], second_parts)
    first_parts = [shifted(first[step], x_axes, step) for step in range(1, 4)]
    second_parts = [shifted(second[step], "z", step) for step in range(1, 4)]
    owned = jnp.stack([added(first[0], first_parts), added(second[0], second_parts)], axis=1)
    return owned[None]


def solution(mesh):
    fine = Mesh(mesh.devices.reshape(2, 2, YS, 2, 4), KA_AXES + BAND_AXES)
    return jax.shard_map(
        local,
        mesh=fine,
        in_specs=(
            P(KA_AXES, None, None, None),
            P(KA_AXES, None),
            P(KA_AXES, BAND_AXES, None, None),
            P(KA_AXES, BAND_AXES),
            P(),
            P(KA_AXES, None),
            P(),
            P(),
        ),
        out_specs=P(None, KA_AXES + BAND_AXES, None, None),
        check_vma=False,
    )
```

```python
import functools

import jax
import jax.numpy as jnp
import numpy as np
from jax import lax
from jax.experimental import pallas as pl
from jax.experimental.pallas import tpu as pltpu
from jax.sharding import Mesh, PartitionSpec as P

GRID = 16
PLANE = GRID * GRID
POINTS = GRID * PLANE
HALF = PLANE // 2
NG = 2048
VB = 64
KA_AXES = ("x_hi", "core")
BAND_AXES = ("y", "x_lo", "z")
KA = 4
BAND = 32
YS = 4
MEMBERS = BAND // YS
CHUNK = 2 * VB
KLOC = 2
DEPTH = YS * 2 * CHUNK
ROWS = 256
OWNERS = ROWS // 16
WIDE = POINTS + 128


def plane_matrices():
    point = np.arange(HALF)
    outer, inner = point // GRID, point % GRID
    parts = []
    for parity in range(2):
        turns = np.outer(2 * outer + parity, outer) + np.outer(inner, inner)
        angle = 2.0 * np.pi * (turns % GRID) / GRID
        cos, sin = np.cos(angle), np.sin(angle)
        parts.append(np.block([[cos, sin], [-sin, cos]]))
    whole = np.stack(parts).astype(np.float32)
    high = whole.astype(jnp.bfloat16)
    low = (whole - high.astype(np.float32)).astype(jnp.bfloat16)
    return high, low


def split(value):
    high = value.astype(jnp.bfloat16)
    low = (value - high.astype(jnp.float32)).astype(jnp.bfloat16)
    return high, low


def four(points):
    (ar, ai), (br, bi), (cr, ci), (dr, di) = points
    sr, si = ar + cr, ai + ci
    tr, ti = ar - cr, ai - ci
    ur, ui = br + dr, bi + di
    wr, wi = br - dr, bi - di
    return [(sr + ur, si + ui), (tr + wi, ti - wr), (sr - ur, si - ui), (tr - wi, ti + wr)]


def turned(point, power):
    re, im = point
    power %= GRID
    if power == 0:
        return re, im
    if power == 4:
        return im, -re
    if power == 2:
        root = float(np.sqrt(0.5))
        return (re + im) * root, (im - re) * root
    if power == 6:
        root = float(np.sqrt(0.5))
        return (im - re) * root, (re + im) * -root
    cos = float(np.cos(2 * np.pi * power / GRID))
    sin = float(np.sin(2 * np.pi * power / GRID))
    return re * cos + im * sin, im * cos - re * sin


def dot_t(left, right):
    return lax.dot_general(left, right, (((1,), (1,)), ((), ())), preferred_element_type=jnp.float32)


def kernel(
    place_ref, sym_ref, rows_ref, occ_hbm, own_hbm, one_hbm, two_hbm, three_hbm, weight_ref, level_ref, whi_hbm, wlo_hbm, near_hbm, far_hbm,
    occ_ref, emp_ref, whi_ref, wlo_ref, mid_ref, xhi0_ref, xlo0_ref, xhi1_ref, xlo1_ref, spec_ref, left_ref,
    pick0_ref, pick1_ref, pick2_ref, pick3_ref, pick4_ref, pick5_ref, pick6_ref, pick7_ref, bhi0_ref, blo0_ref, bhi1_ref, blo1_ref,
    ahi0_ref, alo0_ref, ahi1_ref, alo1_ref, near_ref, far_ref, fac_ref, idx_ref, occ_sems, in_sems, out_sems,
):
    slots = ((xhi0_ref, xlo0_ref), (xhi1_ref, xlo1_ref))
    picks = (pick0_ref, pick1_ref, pick2_ref, pick3_ref, pick4_ref, pick5_ref, pick6_ref, pick7_ref)
    rights = ((bhi0_ref, blo0_ref), (bhi1_ref, blo1_ref))
    lefts = ((ahi0_ref, alo0_ref), (ahi1_ref, alo1_ref))
    copies = [
        [pltpu.make_async_copy(occ_hbm.at[k, :, part], occ_ref.at[k, part], occ_sems.at[k, part]) for part in range(2)]
        for k in range(KLOC)
    ]
    lines = [
        pltpu.make_async_copy(source, emp_ref.at[:, step], in_sems.at[2 + step])
        for step, source in enumerate((own_hbm, one_hbm, two_hbm, three_hbm))
    ]
    others = lines + [
        pltpu.make_async_copy(source, target, in_sems.at[which])
        for which, (source, target) in enumerate(((whi_hbm, whi_ref), (wlo_hbm, wlo_ref)))
    ]
    for copy in lines + copies[0] + others[YS:] + copies[1]:
        copy.start()

    def pairs(step, block, slot):
        xhi_ref, xlo_ref = slots[slot]
        k = step // YS
        band = block // (VB // 16)
        start = pl.multiple_of((block % (VB // 16)) * 16, 16)
        chunk = step % YS

        def pair(a, half):
            base = a * PLANE + half * HALF
            o_re = occ_ref[k, 0, pl.ds(start, 16), pl.ds(base, HALF)]
            o_im = occ_ref[k, 1, pl.ds(start, 16), pl.ds(base, HALF)]
            e_re = emp_ref[k, chunk, band, 0:1, pl.ds(base, HALF)]
            e_im = emp_ref[k, chunk, band, 1:2, pl.ds(base, HALF)]
            return o_re * e_re + o_im * e_im, o_re * e_im - o_im * e_re

        for a0 in range(4):
            even, odd = [], []
            for a1 in range(4):
                fr, fi = pair(4 * a1 + a0, 0)
                sr, si = pair(4 * a1 + a0, 1)
                even.append((fr + sr, fi + si))
                odd.append((fr - sr, fi - si))
            for parity, points in enumerate((even, odd)):
                for k0, point in enumerate(four(points)):
                    re, im = turned(point, a0 * k0)
                    mid_ref[parity, k0, a0, 0] = re
                    mid_ref[parity, k0, a0, 1] = im
        row = pl.multiple_of(block * 16, 16)
        for parity in range(2):
            for k0 in range(4):
                points = [(mid_ref[parity, k0, a0, 0], mid_ref[parity, k0, a0, 1]) for a0 in range(4)]
                for k1, point in enumerate(four(points)):
                    at = k0 + 4 * k1
                    for part in range(2):
                        high, low = split(point[part])
                        xhi_ref[parity, pl.ds(at * CHUNK + row, 16), pl.ds(part * HALF, HALF)] = high
                        xlo_ref[parity, pl.ds(at * CHUNK + row, 16), pl.ds(part * HALF, HALF)] = low

    def places(step, block):
        base = (step * 8 + block) * 64
        shift = rows_ref[ROWS // 8 + step // YS]
        for lane in range(64):
            idx_ref[base + lane] = (place_ref[sym_ref[base + lane]] + shift) & (POINTS * 8 - 1)

    def planes(step, tile, slot):
        xhi_ref, xlo_ref = slots[slot]
        chunk = step % YS
        for parity in range(2):
            at = pl.ds(pl.multiple_of(tile * 2 * CHUNK, 2 * CHUNK), 2 * CHUNK)
            xhi = xhi_ref[parity, at, :]
            xlo = xlo_ref[parity, at, :]
            whi = whi_ref[parity]
            wide = dot_t(jnp.concatenate([whi, wlo_ref[parity]], axis=0), xhi)
            out = dot_t(whi, xlo) + wide[:PLANE] + wide[PLANE:]
            for which in range(2):
                base = ((tile * 2 + which) * PLANE + parity * HALF) * 8 + chunk * 2
                for part in range(2):
                    spec_ref[pl.ds(base + part, HALF, stride=8), :] = out[
                        part * HALF : (part + 1) * HALF, which * CHUNK : (which + 1) * CHUNK
                    ]

    def columns(slot):
        return pl.ds(slot * CHUNK, CHUNK)

    def pick(k, at, to_ref, to):
        source = pl.multiple_of(idx_ref[k * NG + at], 8)
        to_ref[pl.ds(to, 8), :] = spec_ref[pl.ds(source, 8), :]

    def gather_left(k):
        ahi_ref, alo_ref = lefts[k]
        lane = lax.broadcasted_iota(jnp.int32, (1, CHUNK), 1)
        for chunk in range(YS):
            levels = [emp_ref[k, chunk, band, 0:1, POINTS : POINTS + CHUNK] for band in range(2)]
            gap = jnp.where(lane < VB, levels[0], levels[1]) - level_ref[k : k + 1, :]
            fac_ref[chunk : chunk + 1, :] = weight_ref[k * YS + chunk : k * YS + chunk + 1, :] / gap

        def left(step, carry):
            row = pl.multiple_of(step * 16, 16)
            for lane in range(16):
                pick(k, rows_ref[step * 2 + lane // 8] + lane % 8, left_ref, lane * 8)
            for chunk in range(YS):
                factor = fac_ref[chunk : chunk + 1, :]
                re = left_ref[pl.ds(2 * chunk, 16, stride=8), :] * factor
                im = left_ref[pl.ds(2 * chunk + 1, 16, stride=8), :] * factor
                rhi, rlo = split(re)
                ihi, ilo = split(im)
                first, second = columns(2 * chunk), columns(2 * chunk + 1)
                ahi_ref[pl.ds(row, 16), first] = rhi
                alo_ref[pl.ds(row, 16), first] = rlo
                ahi_ref[pl.ds(row, 16), second] = ihi
                alo_ref[pl.ds(row, 16), second] = ilo
                ahi_ref[pl.ds(ROWS + row, 16), first] = -ihi
                alo_ref[pl.ds(ROWS + row, 16), first] = -ilo
                ahi_ref[pl.ds(ROWS + row, 16), second] = rhi
                alo_ref[pl.ds(ROWS + row, 16), second] = rlo
            return carry

        lax.fori_loop(0, ROWS // 16, left, 0)

    def gather(k):
        bhi_ref, blo_ref = rights[k]
        gather_left(k)

        def right(step, carry):
            for which, pick_ref in enumerate(picks):
                row = pl.multiple_of(step * (16 * len(picks)) + which * 16, 16)
                for lane in range(16):
                    pick(k, row + lane, pick_ref, lane * 8)
                for slot in range(8):
                    high, low = split(pick_ref[pl.ds(slot, 16, stride=8), :])
                    bhi_ref[pl.ds(row, 16), columns(slot)] = high
                    blo_ref[pl.ds(row, 16), columns(slot)] = low
            return carry

        lax.fori_loop(0, NG // (16 * len(picks)), right, 0)

    def product(k, at):
        (ahi_ref, alo_ref), (bhi_ref, blo_ref) = lefts[k], rights[k]
        bhi = bhi_ref[at, :]
        ahi = ahi_ref[...]
        return dot_t(ahi, bhi) + dot_t(ahi, blo_ref[at, :]) + dot_t(alo_ref[...], bhi)

    def first(block, carry):
        pairs(0, block, 0)
        places(0, block)
        return carry

    def both(step, slot):
        def body(turn, carry):
            for part in range(2):
                planes(step - 1, turn * 2 + part, 1 - slot)
                pairs(step, turn * 2 + part, slot)
                places(step, turn * 2 + part)
            return carry

        lax.fori_loop(0, 4, body, 0)

    def last(block, carry):
        for part in range(4):
            planes(KLOC * YS - 1, block * 4 + part, 1)
        return carry

    for copy in copies[0] + others:
        copy.wait()
    lax.fori_loop(0, 8, first, 0)

    def two(turn, carry):
        both(2 * turn + 1, 1)

        @pl.when(turn == 1)
        def _():
            for copy in copies[1]:
                copy.wait()

        both(2 * turn + 2, 0)

        @pl.when(turn == 1)
        def _():
            gather(0)

        return carry

    lax.fori_loop(0, 3, two, 0)
    both(KLOC * YS - 1, 1)
    lax.fori_loop(0, 2, last, 0)
    gather(1)

    def places_of(tile):
        return pl.ds(pl.multiple_of(tile * 256, 256), 256)

    def sent(tile):
        return [
            pltpu.make_async_copy(
                source.at[:, :, :, places_of(tile)], target.at[:, :, :, places_of(tile)], out_sems.at[tile, which]
            )
            for which, (source, target) in enumerate(((near_ref, near_hbm), (far_ref, far_hbm)))
        ]

    def one_column(tile):
        out = product(0, places_of(tile)) + product(1, places_of(tile))
        for part in range(2):
            for to in range(OWNERS):
                row = part * ROWS + to * 8
                near_ref[to, part, :, places_of(tile)] = out[row : row + 8]
                far_ref[to, part, :, places_of(tile)] = out[row + ROWS // 2 : row + ROWS // 2 + 8]
        for copy in sent(tile):
            copy.start()

    def columns_of(turn, carry):
        for part in range(2):
            one_column(turn * 2 + part)
        return carry

    def done(tile, carry):
        for copy in sent(tile):
            copy.wait()
        return carry

    lax.fori_loop(0, NG // 256 // 2, columns_of, 0)
    lax.fori_loop(0, NG // 256, done, 0)


def partial_rows(places, sym_map, rows, occ, emp, strength, level):
    whi, wlo = plane_matrices()
    vmem = pl.BlockSpec(memory_space=pltpu.VMEM)
    smem = pl.BlockSpec(memory_space=pltpu.SMEM)
    hbm = pl.BlockSpec(memory_space=pl.ANY)
    part = jax.ShapeDtypeStruct((OWNERS, 2, 8, NG), jnp.float32)
    return pl.pallas_call(
        kernel,
        out_shape=(part, part),
        in_specs=[smem, smem, smem] + [hbm] * 5 + [vmem, vmem, hbm, hbm],
        out_specs=(hbm, hbm),
        scratch_shapes=[
            pltpu.VMEM((KLOC, 2, VB, POINTS), jnp.float32),
            pltpu.VMEM((KLOC, YS, 2, 2, WIDE), jnp.float32),
            pltpu.VMEM((2, PLANE, PLANE), jnp.bfloat16),
            pltpu.VMEM((2, PLANE, PLANE), jnp.bfloat16),
            pltpu.VMEM((2, 4, 4, 2, 16, HALF), jnp.float32),
        ]
        + [pltpu.VMEM((2, GRID * CHUNK, PLANE), jnp.bfloat16)] * 4
        + [pltpu.VMEM((POINTS * 8, CHUNK), jnp.float32)]
        + [pltpu.VMEM((16 * 8, CHUNK), jnp.float32)] * 9
        + [pltpu.VMEM((NG, DEPTH), jnp.bfloat16)] * 4
        + [pltpu.VMEM((2 * ROWS, DEPTH), jnp.bfloat16)] * 4
        + [pltpu.VMEM((OWNERS, 2, 8, NG), jnp.float32)] * 2
        + [
            pltpu.VMEM((8, CHUNK), jnp.float32),
            pltpu.SMEM((KLOC * NG,), jnp.int32),
            pltpu.SemaphoreType.DMA((KLOC, 2)),
            pltpu.SemaphoreType.DMA((2 + YS,)),
            pltpu.SemaphoreType.DMA((NG // 256, 2)),
        ],
        compiler_params=pltpu.CompilerParams(vmem_limit_bytes=62 * 2**20),
        cost_estimate=pl.CostEstimate(flops=40 * 10**9, bytes_accessed=10 * 2**20, transcendentals=0),
    )(places, sym_map, rows, occ, *emp, strength, level, jnp.asarray(whi), jnp.asarray(wlo))


def shifted(value, axis, by):
    size = lax.axis_size(axis)
    return lax.ppermute(value, axis, [(index, (index + by) % size) for index in range(size)])


def local(occ_orb, occ_energy, emp_orb, emp_energy, gidx, sym_map, weights, count):
    ka = lax.axis_index(KA_AXES)
    core = lax.axis_index("core")
    y = lax.axis_index("y")
    member = lax.axis_index(("x_lo", "z"))

    spread = jnp.pad(emp_orb, ((0, 0), (0, 0), (0, 0), (0, WIDE - POINTS)))
    lane = lax.broadcasted_iota(jnp.int32, spread.shape, 3)
    lines = jnp.where(lane < POINTS, spread, emp_energy[:, :, None, None])
    own = jnp.stack([lines[1], shifted(lines[0], KA_AXES, -1)])
    emp = [own] + [shifted(own, "y", -step) for step in range(1, YS)]

    kpoint = ka * KLOC + jnp.arange(KLOC, dtype=jnp.int32)
    wrapped = (kpoint + 1 >= KA * KLOC).astype(jnp.int32)
    target = kpoint + 1 - wrapped * (KA * KLOC)
    odd = (gidx // GRID) % 2
    outer = (gidx // (2 * GRID)) % 8
    places = (gidx // PLANE * PLANE + odd * HALF + outer * GRID + gidx % GRID) * 8

    wsum = jnp.sum(weights).astype(jnp.float32)
    scale = -4.0 / jnp.sqrt(jnp.float32(VB * 2 * BAND) * wsum) / POINTS
    owner = (y + jnp.arange(YS, dtype=jnp.int32)) % YS
    bands = owner[:, None] * (2 * MEMBERS) + member * 2 + jnp.arange(2, dtype=jnp.int32)[None, :]
    live = (bands[None] < count[target][:, None, None]).astype(jnp.float32)
    strength = (scale * weights[kpoint].astype(jnp.float32))[:, None, None, None]
    strength = jnp.broadcast_to(strength * live[..., None], (KLOC, YS, 2, VB)).reshape(KLOC * YS, CHUNK)
    level = jnp.concatenate([occ_energy, occ_energy], axis=1)

    near_core = jnp.arange(2, dtype=jnp.int32)[:, None, None]
    x = lax.axis_index(("x_hi", "x_lo"))
    z = lax.axis_index("z")
    to_x = (x + jnp.arange(4, dtype=jnp.int32)[None, :, None]) % 4
    to_z = (z + jnp.arange(4, dtype=jnp.int32)[None, None, :]) % 4
    to_ka = (to_x // 2) * 2 + (core + near_core) % 2
    rows = (to_ka * 256 + y * 64 + (to_x % 2) * 32 + to_z * 8).reshape(32)
    rows = jnp.concatenate([rows, wrapped * (PLANE * 8)])

    near, far = partial_rows(places, sym_map.reshape(KLOC * NG), rows.astype(jnp.int32), occ_orb, emp, strength, level)

    both = near + shifted(far, "core", 1)
    both = both.reshape(4, 4, 2, 8, NG)
    x_axes = ("x_hi", "x_lo")

    def added(own, parts):
        return own + (parts[0] + parts[1]) + parts[2]

    first, second = both[:, :, 0], both[:, :, 1]
    first_parts = [shifted(first[:, step], "z", step) for step in range(1, 4)]
    second_parts = [shifted(second[step], x_axes, step) for step in range(1, 4)]
    first = added(first[:, 0], first_parts)
    second = added(second[0], second_parts)
    first_parts = [shifted(first[step], x_axes, step) for step in range(1, 4)]
    second_parts = [shifted(second[step], "z", step) for step in range(1, 4)]
    owned = jnp.stack([added(first[0], first_parts), added(second[0], second_parts)], axis=1)
    return owned[None]


def solution(mesh):
    fine = Mesh(mesh.devices.reshape(2, 2, YS, 2, 4), KA_AXES + BAND_AXES)
    return jax.shard_map(
        local,
        mesh=fine,
        in_specs=(
            P(KA_AXES, None, None, None),
            P(KA_AXES, None),
            P(KA_AXES, BAND_AXES, None, None),
            P(KA_AXES, BAND_AXES),
            P(),
            P(KA_AXES, None),
            P(),
            P(),
        ),
        out_specs=P(None, KA_AXES + BAND_AXES, None, None),
        check_vma=False,
    )
```

```python
import functools

import jax
import jax.numpy as jnp
import numpy as np
from jax import lax
from jax.experimental import pallas as pl
from jax.experimental.pallas import tpu as pltpu
from jax.sharding import Mesh, PartitionSpec as P

GRID = 16
PLANE = GRID * GRID
POINTS = GRID * PLANE
HALF = PLANE // 2
NG = 2048
VB = 64
KA_AXES = ("x_hi", "core")
BAND_AXES = ("y", "x_lo", "z")
KA = 4
BAND = 32
YS = 4
MEMBERS = BAND // YS
CHUNK = 2 * VB
KLOC = 2
DEPTH = YS * 2 * CHUNK
ROWS = 256
OWNERS = ROWS // 16
WIDE = POINTS + 128


def plane_matrices():
    point = np.arange(HALF)
    outer, inner = point // GRID, point % GRID
    parts = []
    for parity in range(2):
        turns = np.outer(2 * outer + parity, outer) + np.outer(inner, inner)
        angle = 2.0 * np.pi * (turns % GRID) / GRID
        cos, sin = np.cos(angle), np.sin(angle)
        parts.append(np.block([[cos, sin], [-sin, cos]]))
    whole = np.stack(parts).astype(np.float32)
    high = whole.astype(jnp.bfloat16)
    low = (whole - high.astype(np.float32)).astype(jnp.bfloat16)
    return high, low


def split(value):
    high = value.astype(jnp.bfloat16)
    low = (value - high.astype(jnp.float32)).astype(jnp.bfloat16)
    return high, low


def four(points):
    (ar, ai), (br, bi), (cr, ci), (dr, di) = points
    sr, si = ar + cr, ai + ci
    tr, ti = ar - cr, ai - ci
    ur, ui = br + dr, bi + di
    wr, wi = br - dr, bi - di
    return [(sr + ur, si + ui), (tr + wi, ti - wr), (sr - ur, si - ui), (tr - wi, ti + wr)]


def turned(point, power):
    re, im = point
    power %= GRID
    if power == 0:
        return re, im
    if power == 4:
        return im, -re
    if power == 2:
        root = float(np.sqrt(0.5))
        return (re + im) * root, (im - re) * root
    if power == 6:
        root = float(np.sqrt(0.5))
        return (im - re) * root, (re + im) * -root
    cos = float(np.cos(2 * np.pi * power / GRID))
    sin = float(np.sin(2 * np.pi * power / GRID))
    return re * cos + im * sin, im * cos - re * sin


def dot_t(left, right):
    return lax.dot_general(left, right, (((1,), (1,)), ((), ())), preferred_element_type=jnp.float32)


def kernel(
    place_ref, sym_ref, rows_ref, occ_hbm, own_hbm, one_hbm, two_hbm, three_hbm, weight_ref, level_ref, whi_hbm, wlo_hbm, near_hbm, far_hbm,
    occ_ref, emp_ref, whi_ref, wlo_ref, mid_ref, xhi0_ref, xlo0_ref, xhi1_ref, xlo1_ref, spec_ref, left_ref,
    pick0_ref, pick1_ref, pick2_ref, pick3_ref, pick4_ref, pick5_ref, pick6_ref, pick7_ref, bhi0_ref, blo0_ref, bhi1_ref, blo1_ref,
    ahi0_ref, alo0_ref, ahi1_ref, alo1_ref, near_ref, far_ref, fac_ref, idx_ref, occ_sems, in_sems, out_sems,
):
    slots = ((xhi0_ref, xlo0_ref), (xhi1_ref, xlo1_ref))
    picks = (pick0_ref, pick1_ref, pick2_ref, pick3_ref, pick4_ref, pick5_ref, pick6_ref, pick7_ref)
    rights = ((bhi0_ref, blo0_ref), (bhi1_ref, blo1_ref))
    lefts = ((ahi0_ref, alo0_ref), (ahi1_ref, alo1_ref))
    copies = [
        [pltpu.make_async_copy(occ_hbm.at[k, :, part], occ_ref.at[k, part], occ_sems.at[k, part]) for part in range(2)]
        for k in range(KLOC)
    ]
    lines = [
        pltpu.make_async_copy(source, emp_ref.at[:, step], in_sems.at[2 + step])
        for step, source in enumerate((own_hbm, one_hbm, two_hbm, three_hbm))
    ]
    others = lines + [
        pltpu.make_async_copy(source, target, in_sems.at[which])
        for which, (source, target) in enumerate(((whi_hbm, whi_ref), (wlo_hbm, wlo_ref)))
    ]
    for copy in lines + copies[0] + others[YS:] + copies[1]:
        copy.start()

    def pairs(step, block, slot):
        xhi_ref, xlo_ref = slots[slot]
        k = step // YS
        band = block // (VB // 16)
        start = pl.multiple_of((block % (VB // 16)) * 16, 16)
        chunk = step % YS

        def pair(a, half):
            base = a * PLANE + half * HALF
            o_re = occ_ref[k, 0, pl.ds(start, 16), pl.ds(base, HALF)]
            o_im = occ_ref[k, 1, pl.ds(start, 16), pl.ds(base, HALF)]
            e_re = emp_ref[k, chunk, band, 0:1, pl.ds(base, HALF)]
            e_im = emp_ref[k, chunk, band, 1:2, pl.ds(base, HALF)]
            return o_re * e_re + o_im * e_im, o_re * e_im - o_im * e_re

        for a0 in range(4):
            even, odd = [], []
            for a1 in range(4):
                fr, fi = pair(4 * a1 + a0, 0)
                sr, si = pair(4 * a1 + a0, 1)
                even.append((fr + sr, fi + si))
                odd.append((fr - sr, fi - si))
            for parity, points in enumerate((even, odd)):
                for k0, point in enumerate(four(points)):
                    re, im = turned(point, a0 * k0)
                    mid_ref[parity, k0, a0, 0] = re
                    mid_ref[parity, k0, a0, 1] = im
        row = pl.multiple_of(block * 16, 16)
        for parity in range(2):
            for k0 in range(4):
                points = [(mid_ref[parity, k0, a0, 0], mid_ref[parity, k0, a0, 1]) for a0 in range(4)]
                for k1, point in enumerate(four(points)):
                    at = k0 + 4 * k1
                    for part in range(2):
                        high, low = split(point[part])
                        xhi_ref[parity, pl.ds(at * CHUNK + row, 16), pl.ds(part * HALF, HALF)] = high
                        xlo_ref[parity, pl.ds(at * CHUNK + row, 16), pl.ds(part * HALF, HALF)] = low

    def places(step, block):
        base = (step * 8 + block) * 64
        shift = rows_ref[ROWS // 8 + step // YS]
        for lane in range(64):
            idx_ref[base + lane] = (place_ref[sym_ref[base + lane]] + shift) & (POINTS * 8 - 1)

    def planes(step, tile, slot):
        xhi_ref, xlo_ref = slots[slot]
        chunk = step % YS
        for parity in range(2):
            at = pl.ds(pl.multiple_of(tile * 2 * CHUNK, 2 * CHUNK), 2 * CHUNK)
            xhi = xhi_ref[parity, at, :]
            xlo = xlo_ref[parity, at, :]
            whi = whi_ref[parity]
            wide = dot_t(jnp.concatenate([whi, wlo_ref[parity]], axis=0), xhi)
            out = dot_t(whi, xlo) + wide[:PLANE] + wide[PLANE:]
            for which in range(2):
                base = ((tile * 2 + which) * PLANE + parity * HALF) * 8 + chunk * 2
                for part in range(2):
                    spec_ref[pl.ds(base + part, HALF, stride=8), :] = out[
                        part * HALF : (part + 1) * HALF, which * CHUNK : (which + 1) * CHUNK
                    ]

    def columns(slot):
        return pl.ds(slot * CHUNK, CHUNK)

    def pick(k, at, to_ref, to):
        source = pl.multiple_of(idx_ref[k * NG + at], 8)
        to_ref[pl.ds(to, 8), :] = spec_ref[pl.ds(source, 8), :]

    def gather_left(k):
        ahi_ref, alo_ref = lefts[k]
        lane = lax.broadcasted_iota(jnp.int32, (1, CHUNK), 1)
        for chunk in range(YS):
            levels = [emp_ref[k, chunk, band, 0:1, POINTS : POINTS + CHUNK] for band in range(2)]
            gap = jnp.where(lane < VB, levels[0], levels[1]) - level_ref[k : k + 1, :]
            fac_ref[chunk : chunk + 1, :] = weight_ref[k * YS + chunk : k * YS + chunk + 1, :] / gap

        def left(step, carry):
            row = pl.multiple_of(step * 16, 16)
            for lane in range(16):
                pick(k, rows_ref[step * 2 + lane // 8] + lane % 8, left_ref, lane * 8)
            for chunk in range(YS):
                factor = fac_ref[chunk : chunk + 1, :]
                re = left_ref[pl.ds(2 * chunk, 16, stride=8), :] * factor
                im = left_ref[pl.ds(2 * chunk + 1, 16, stride=8), :] * factor
                rhi, rlo = split(re)
                ihi, ilo = split(im)
                first, second = columns(2 * chunk), columns(2 * chunk + 1)
                ahi_ref[pl.ds(row, 16), first] = rhi
                alo_ref[pl.ds(row, 16), first] = rlo
                ahi_ref[pl.ds(row, 16), second] = ihi
                alo_ref[pl.ds(row, 16), second] = ilo
                ahi_ref[pl.ds(ROWS + row, 16), first] = -ihi
                alo_ref[pl.ds(ROWS + row, 16), first] = -ilo
                ahi_ref[pl.ds(ROWS + row, 16), second] = rhi
                alo_ref[pl.ds(ROWS + row, 16), second] = rlo
            return carry

        lax.fori_loop(0, ROWS // 16, left, 0)

    def gather(k):
        bhi_ref, blo_ref = rights[k]
        gather_left(k)

        def right(step, carry):
            for which, pick_ref in enumerate(picks):
                row = pl.multiple_of(step * (16 * len(picks)) + which * 16, 16)
                for lane in range(16):
                    pick(k, row + lane, pick_ref, lane * 8)
                for slot in range(8):
                    high, low = split(pick_ref[pl.ds(slot, 16, stride=8), :])
                    bhi_ref[pl.ds(row, 16), columns(slot)] = high
                    blo_ref[pl.ds(row, 16), columns(slot)] = low
            return carry

        lax.fori_loop(0, NG // (16 * len(picks)), right, 0)

    def product(k, at):
        (ahi_ref, alo_ref), (bhi_ref, blo_ref) = lefts[k], rights[k]
        bhi = bhi_ref[at, :]
        ahi = ahi_ref[...]
        return dot_t(ahi, bhi) + dot_t(ahi, blo_ref[at, :]) + dot_t(alo_ref[...], bhi)

    def first(block, carry):
        pairs(0, block, 0)
        places(0, block)
        return carry

    def both(step, slot):
        def body(turn, carry):
            for part in range(2):
                planes(step - 1, turn * 2 + part, 1 - slot)
                pairs(step, turn * 2 + part, slot)
                places(step, turn * 2 + part)
            return carry

        lax.fori_loop(0, 4, body, 0)

    def last(block, carry):
        for part in range(4):
            planes(KLOC * YS - 1, block * 4 + part, 1)
        return carry

    for copy in copies[0] + others:
        copy.wait()
    lax.fori_loop(0, 8, first, 0)

    def two(turn, carry):
        both(2 * turn + 1, 1)

        @pl.when(turn == 1)
        def _():
            for copy in copies[1]:
                copy.wait()

        both(2 * turn + 2, 0)

        @pl.when(turn == 1)
        def _():
            gather(0)

        return carry

    lax.fori_loop(0, 3, two, 0)
    both(KLOC * YS - 1, 1)
    lax.fori_loop(0, 2, last, 0)
    gather(1)

    def places_of(tile):
        return pl.ds(pl.multiple_of(tile * 256, 256), 256)

    def sent(tile):
        return [
            pltpu.make_async_copy(
                source.at[:, :, :, places_of(tile)], target.at[:, :, :, places_of(tile)], out_sems.at[tile, which]
            )
            for which, (source, target) in enumerate(((near_ref, near_hbm), (far_ref, far_hbm)))
        ]

    def one_column(tile):
        out = product(0, places_of(tile)) + product(1, places_of(tile))
        for part in range(2):
            for to in range(OWNERS):
                row = part * ROWS + to * 8
                near_ref[to, part, :, places_of(tile)] = out[row : row + 8]
                far_ref[to, part, :, places_of(tile)] = out[row + ROWS // 2 : row + ROWS // 2 + 8]
        for copy in sent(tile):
            copy.start()

    def columns_of(turn, carry):
        for part in range(2):
            one_column(turn * 2 + part)
        return carry

    def done(tile, carry):
        for copy in sent(tile):
            copy.wait()
        return carry

    lax.fori_loop(0, NG // 256 // 2, columns_of, 0)
    lax.fori_loop(0, NG // 256, done, 0)


def partial_rows(places, sym_map, rows, occ, emp, strength, level):
    whi, wlo = plane_matrices()
    vmem = pl.BlockSpec(memory_space=pltpu.VMEM)
    smem = pl.BlockSpec(memory_space=pltpu.SMEM)
    hbm = pl.BlockSpec(memory_space=pl.ANY)
    part = jax.ShapeDtypeStruct((OWNERS, 2, 8, NG), jnp.float32)
    return pl.pallas_call(
        kernel,
        out_shape=(part, part),
        in_specs=[smem, smem, smem] + [hbm] * 5 + [vmem, vmem, hbm, hbm],
        out_specs=(hbm, hbm),
        scratch_shapes=[
            pltpu.VMEM((KLOC, 2, VB, POINTS), jnp.float32),
            pltpu.VMEM((KLOC, YS, 2, 2, WIDE), jnp.float32),
            pltpu.VMEM((2, PLANE, PLANE), jnp.bfloat16),
            pltpu.VMEM((2, PLANE, PLANE), jnp.bfloat16),
            pltpu.VMEM((2, 4, 4, 2, 16, HALF), jnp.float32),
        ]
        + [pltpu.VMEM((2, GRID * CHUNK, PLANE), jnp.bfloat16)] * 4
        + [pltpu.VMEM((POINTS * 8 + 8, CHUNK), jnp.float32)]
        + [pltpu.VMEM((16 * 8 + 8, CHUNK), jnp.float32)] * 9
        + [pltpu.VMEM((NG, DEPTH), jnp.bfloat16)] * 4
        + [pltpu.VMEM((2 * ROWS, DEPTH), jnp.bfloat16)] * 4
        + [pltpu.VMEM((OWNERS, 2, 8, NG), jnp.float32)] * 2
        + [
            pltpu.VMEM((8, CHUNK), jnp.float32),
            pltpu.SMEM((KLOC * NG,), jnp.int32),
            pltpu.SemaphoreType.DMA((KLOC, 2)),
            pltpu.SemaphoreType.DMA((2 + YS,)),
            pltpu.SemaphoreType.DMA((NG // 256, 2)),
        ],
        compiler_params=pltpu.CompilerParams(vmem_limit_bytes=62 * 2**20),
        cost_estimate=pl.CostEstimate(flops=40 * 10**9, bytes_accessed=10 * 2**20, transcendentals=0),
    )(places, sym_map, rows, occ, *emp, strength, level, jnp.asarray(whi), jnp.asarray(wlo))


def shifted(value, axis, by):
    size = lax.axis_size(axis)
    return lax.ppermute(value, axis, [(index, (index + by) % size) for index in range(size)])


def local(occ_orb, occ_energy, emp_orb, emp_energy, gidx, sym_map, weights, count):
    ka = lax.axis_index(KA_AXES)
    core = lax.axis_index("core")
    y = lax.axis_index("y")
    member = lax.axis_index(("x_lo", "z"))

    spread = jnp.pad(emp_orb, ((0, 0), (0, 0), (0, 0), (0, WIDE - POINTS)))
    lane = lax.broadcasted_iota(jnp.int32, spread.shape, 3)
    lines = jnp.where(lane < POINTS, spread, emp_energy[:, :, None, None])
    own = jnp.stack([lines[1], shifted(lines[0], KA_AXES, -1)])
    emp = [own] + [shifted(own, "y", -step) for step in range(1, YS)]

    kpoint = ka * KLOC + jnp.arange(KLOC, dtype=jnp.int32)
    wrapped = (kpoint + 1 >= KA * KLOC).astype(jnp.int32)
    target = kpoint + 1 - wrapped * (KA * KLOC)
    odd = (gidx // GRID) % 2
    outer = (gidx // (2 * GRID)) % 8
    places = (gidx // PLANE * PLANE + odd * HALF + outer * GRID + gidx % GRID) * 8

    wsum = jnp.sum(weights).astype(jnp.float32)
    scale = -4.0 / jnp.sqrt(jnp.float32(VB * 2 * BAND) * wsum) / POINTS
    owner = (y + jnp.arange(YS, dtype=jnp.int32)) % YS
    bands = owner[:, None] * (2 * MEMBERS) + member * 2 + jnp.arange(2, dtype=jnp.int32)[None, :]
    live = (bands[None] < count[target][:, None, None]).astype(jnp.float32)
    strength = (scale * weights[kpoint].astype(jnp.float32))[:, None, None, None]
    strength = jnp.broadcast_to(strength * live[..., None], (KLOC, YS, 2, VB)).reshape(KLOC * YS, CHUNK)
    level = jnp.concatenate([occ_energy, occ_energy], axis=1)

    near_core = jnp.arange(2, dtype=jnp.int32)[:, None, None]
    x = lax.axis_index(("x_hi", "x_lo"))
    z = lax.axis_index("z")
    to_x = (x + jnp.arange(4, dtype=jnp.int32)[None, :, None]) % 4
    to_z = (z + jnp.arange(4, dtype=jnp.int32)[None, None, :]) % 4
    to_ka = (to_x // 2) * 2 + (core + near_core) % 2
    rows = (to_ka * 256 + y * 64 + (to_x % 2) * 32 + to_z * 8).reshape(32)
    rows = jnp.concatenate([rows, wrapped * (PLANE * 8)])

    near, far = partial_rows(places, sym_map.reshape(KLOC * NG), rows.astype(jnp.int32), occ_orb, emp, strength, level)

    both = near + shifted(far, "core", 1)
    both = both.reshape(4, 4, 2, 8, NG)
    x_axes = ("x_hi", "x_lo")

    def added(own, parts):
        return own + (parts[0] + parts[1]) + parts[2]

    first, second = both[:, :, 0], both[:, :, 1]
    first_parts = [shifted(first[:, step], "z", step) for step in range(1, 4)]
    second_parts = [shifted(second[step], x_axes, step) for step in range(1, 4)]
    first = added(first[:, 0], first_parts)
    second = added(second[0], second_parts)
    first_parts = [shifted(first[step], x_axes, step) for step in range(1, 4)]
    second_parts = [shifted(second[step], "z", step) for step in range(1, 4)]
    owned = jnp.stack([added(first[0], first_parts), added(second[0], second_parts)], axis=1)
    return owned[None]


def solution(mesh):
    fine = Mesh(mesh.devices.reshape(2, 2, YS, 2, 4), KA_AXES + BAND_AXES)
    return jax.shard_map(
        local,
        mesh=fine,
        in_specs=(
            P(KA_AXES, None, None, None),
            P(KA_AXES, None),
            P(KA_AXES, BAND_AXES, None, None),
            P(KA_AXES, BAND_AXES),
            P(),
            P(KA_AXES, None),
            P(),
            P(),
        ),
        out_specs=P(None, KA_AXES + BAND_AXES, None, None),
        check_vma=False,
    )
```

```python
import functools

import jax
import jax.numpy as jnp
import numpy as np
from jax import lax
from jax.experimental import pallas as pl
from jax.experimental.pallas import tpu as pltpu
from jax.sharding import Mesh, PartitionSpec as P

GRID = 16
PLANE = GRID * GRID
POINTS = GRID * PLANE
HALF = PLANE // 2
NG = 2048
VB = 64
KA_AXES = ("x_hi", "core")
BAND_AXES = ("y", "x_lo", "z")
KA = 4
BAND = 32
YS = 4
MEMBERS = BAND // YS
CHUNK = 2 * VB
KLOC = 2
DEPTH = YS * 2 * CHUNK
ROWS = 256
OWNERS = ROWS // 16
WIDE = POINTS + 128


def plane_matrices():
    point = np.arange(HALF)
    outer, inner = point // GRID, point % GRID
    parts = []
    for parity in range(2):
        turns = np.outer(2 * outer + parity, outer) + np.outer(inner, inner)
        angle = 2.0 * np.pi * (turns % GRID) / GRID
        cos, sin = np.cos(angle), np.sin(angle)
        parts.append(np.block([[cos, sin], [-sin, cos]]))
    whole = np.stack(parts).astype(np.float32)
    high = whole.astype(jnp.bfloat16)
    low = (whole - high.astype(np.float32)).astype(jnp.bfloat16)
    return high, low


def split(value):
    high = value.astype(jnp.bfloat16)
    low = (value - high.astype(jnp.float32)).astype(jnp.bfloat16)
    return high, low


def four(points):
    (ar, ai), (br, bi), (cr, ci), (dr, di) = points
    sr, si = ar + cr, ai + ci
    tr, ti = ar - cr, ai - ci
    ur, ui = br + dr, bi + di
    wr, wi = br - dr, bi - di
    return [(sr + ur, si + ui), (tr + wi, ti - wr), (sr - ur, si - ui), (tr - wi, ti + wr)]


def turned(point, power):
    re, im = point
    power %= GRID
    if power == 0:
        return re, im
    if power == 4:
        return im, -re
    if power == 2:
        root = float(np.sqrt(0.5))
        return (re + im) * root, (im - re) * root
    if power == 6:
        root = float(np.sqrt(0.5))
        return (im - re) * root, (re + im) * -root
    cos = float(np.cos(2 * np.pi * power / GRID))
    sin = float(np.sin(2 * np.pi * power / GRID))
    return re * cos + im * sin, im * cos - re * sin


def dot_t(left, right):
    return lax.dot_general(left, right, (((1,), (1,)), ((), ())), preferred_element_type=jnp.float32)


def kernel(
    place_ref, sym_ref, rows_ref, occ_hbm, own_hbm, one_hbm, two_hbm, three_hbm, weight_ref, level_ref, whi_hbm, wlo_hbm, near_hbm, far_hbm,
    occ_ref, emp_ref, whi_ref, wlo_ref, mid_ref, xhi0_ref, xlo0_ref, xhi1_ref, xlo1_ref, spec_ref, left_ref,
    pick0_ref, pick1_ref, pick2_ref, pick3_ref, pick4_ref, pick5_ref, pick6_ref, pick7_ref, bhi0_ref, blo0_ref, bhi1_ref, blo1_ref,
    ahi0_ref, alo0_ref, ahi1_ref, alo1_ref, near_ref, far_ref, fac_ref, idx_ref, occ_sems, in_sems, out_sems,
):
    slots = ((xhi0_ref, xlo0_ref), (xhi1_ref, xlo1_ref))
    picks = (pick0_ref, pick1_ref, pick2_ref, pick3_ref, pick4_ref, pick5_ref, pick6_ref, pick7_ref)
    rights = ((bhi0_ref, blo0_ref), (bhi1_ref, blo1_ref))
    lefts = ((ahi0_ref, alo0_ref), (ahi1_ref, alo1_ref))
    copies = [
        [pltpu.make_async_copy(occ_hbm.at[k, :, part], occ_ref.at[k, part], occ_sems.at[k, part]) for part in range(2)]
        for k in range(KLOC)
    ]
    lines = [
        pltpu.make_async_copy(source, emp_ref.at[:, step], in_sems.at[2 + step])
        for step, source in enumerate((own_hbm, one_hbm, two_hbm, three_hbm))
    ]
    others = lines + [
        pltpu.make_async_copy(source, target, in_sems.at[which])
        for which, (source, target) in enumerate(((whi_hbm, whi_ref), (wlo_hbm, wlo_ref)))
    ]
    for copy in lines + copies[0] + others[YS:] + copies[1]:
        copy.start()

    def pairs(step, block, slot):
        xhi_ref, xlo_ref = slots[slot]
        k = step // YS
        band = block // (VB // 16)
        start = pl.multiple_of((block % (VB // 16)) * 16, 16)
        chunk = step % YS

        def pair(a, half):
            base = a * PLANE + half * HALF
            o_re = occ_ref[k, 0, pl.ds(start, 16), pl.ds(base, HALF)]
            o_im = occ_ref[k, 1, pl.ds(start, 16), pl.ds(base, HALF)]
            e_re = emp_ref[k, chunk, band, 0:1, pl.ds(base, HALF)]
            e_im = emp_ref[k, chunk, band, 1:2, pl.ds(base, HALF)]
            return o_re * e_re + o_im * e_im, o_re * e_im - o_im * e_re

        for a0 in range(4):
            even, odd = [], []
            for a1 in range(4):
                fr, fi = pair(4 * a1 + a0, 0)
                sr, si = pair(4 * a1 + a0, 1)
                even.append((fr + sr, fi + si))
                odd.append((fr - sr, fi - si))
            for parity, points in enumerate((even, odd)):
                for k0, point in enumerate(four(points)):
                    re, im = turned(point, a0 * k0)
                    mid_ref[parity, k0, a0, 0] = re
                    mid_ref[parity, k0, a0, 1] = im
        row = pl.multiple_of(block * 16, 16)
        for parity in range(2):
            for k0 in range(4):
                points = [(mid_ref[parity, k0, a0, 0], mid_ref[parity, k0, a0, 1]) for a0 in range(4)]
                for k1, point in enumerate(four(points)):
                    at = k0 + 4 * k1
                    for part in range(2):
                        high, low = split(point[part])
                        xhi_ref[parity, pl.ds(at * CHUNK + row, 16), pl.ds(part * HALF, HALF)] = high
                        xlo_ref[parity, pl.ds(at * CHUNK + row, 16), pl.ds(part * HALF, HALF)] = low

    def places(step, block):
        base = (step * 8 + block) * 64
        shift = rows_ref[ROWS // 8 + step // YS]
        for lane in range(64):
            idx_ref[base + lane] = (place_ref[sym_ref[base + lane]] + shift) & (POINTS * 8 - 1)

    def planes(step, tile, slot):
        xhi_ref, xlo_ref = slots[slot]
        chunk = step % YS
        for parity in range(2):
            at = pl.ds(pl.multiple_of(tile * 2 * CHUNK, 2 * CHUNK), 2 * CHUNK)
            xhi = xhi_ref[parity, at, :]
            xlo = xlo_ref[parity, at, :]
            whi = whi_ref[parity]
            wide = dot_t(jnp.concatenate([whi, wlo_ref[parity]], axis=0), xhi)
            out = dot_t(whi, xlo) + wide[:PLANE] + wide[PLANE:]
            for which in range(2):
                base = ((tile * 2 + which) * PLANE + parity * HALF) * 8 + chunk * 2
                for part in range(2):
                    spec_ref[pl.ds(base + part, HALF, stride=8), :] = out[
                        part * HALF : (part + 1) * HALF, which * CHUNK : (which + 1) * CHUNK
                    ]

    def columns(slot):
        return pl.ds(slot * CHUNK, CHUNK)

    def pick(k, at, to_ref, to):
        source = pl.multiple_of(idx_ref[k * NG + at], 8)
        to_ref[pl.ds(to, 8), :] = spec_ref[pl.ds(source, 8), :]

    def gather_left(k):
        ahi_ref, alo_ref = lefts[k]
        lane = lax.broadcasted_iota(jnp.int32, (1, CHUNK), 1)
        for chunk in range(YS):
            levels = [emp_ref[k, chunk, band, 0:1, POINTS : POINTS + CHUNK] for band in range(2)]
            gap = jnp.where(lane < VB, levels[0], levels[1]) - level_ref[k : k + 1, :]
            fac_ref[chunk : chunk + 1, :] = weight_ref[k * YS + chunk : k * YS + chunk + 1, :] / gap

        def left(step, carry):
            row = pl.multiple_of(step * 16, 16)
            for lane in range(16):
                pick(k, rows_ref[step * 2 + lane // 8] + lane % 8, left_ref, lane * 8)
            for chunk in range(YS):
                factor = fac_ref[chunk : chunk + 1, :]
                re = left_ref[pl.ds(2 * chunk, 16, stride=8), :] * factor
                im = left_ref[pl.ds(2 * chunk + 1, 16, stride=8), :] * factor
                rhi, rlo = split(re)
                ihi, ilo = split(im)
                first, second = columns(2 * chunk), columns(2 * chunk + 1)
                ahi_ref[pl.ds(row, 16), first] = rhi
                alo_ref[pl.ds(row, 16), first] = rlo
                ahi_ref[pl.ds(row, 16), second] = ihi
                alo_ref[pl.ds(row, 16), second] = ilo
                ahi_ref[pl.ds(ROWS + row, 16), first] = -ihi
                alo_ref[pl.ds(ROWS + row, 16), first] = -ilo
                ahi_ref[pl.ds(ROWS + row, 16), second] = rhi
                alo_ref[pl.ds(ROWS + row, 16), second] = rlo
            return carry

        lax.fori_loop(0, ROWS // 16, left, 0, unroll=2)

    def gather(k):
        bhi_ref, blo_ref = rights[k]
        gather_left(k)

        def right(step, carry):
            for which, pick_ref in enumerate(picks):
                row = pl.multiple_of(step * (16 * len(picks)) + which * 16, 16)
                for lane in range(16):
                    pick(k, row + lane, pick_ref, lane * 8)
                for slot in range(8):
                    high, low = split(pick_ref[pl.ds(slot, 16, stride=8), :])
                    bhi_ref[pl.ds(row, 16), columns(slot)] = high
                    blo_ref[pl.ds(row, 16), columns(slot)] = low
            return carry

        lax.fori_loop(0, NG // (16 * len(picks)), right, 0)

    def product(k, at):
        (ahi_ref, alo_ref), (bhi_ref, blo_ref) = lefts[k], rights[k]
        bhi = bhi_ref[at, :]
        ahi = ahi_ref[...]
        return dot_t(ahi, bhi) + dot_t(ahi, blo_ref[at, :]) + dot_t(alo_ref[...], bhi)

    def first(block, carry):
        pairs(0, block, 0)
        places(0, block)
        return carry

    def both(step, slot):
        def body(turn, carry):
            for part in range(2):
                planes(step - 1, turn * 2 + part, 1 - slot)
                pairs(step, turn * 2 + part, slot)
                places(step, turn * 2 + part)
            return carry

        lax.fori_loop(0, 4, body, 0)

    def last(block, carry):
        for part in range(4):
            planes(KLOC * YS - 1, block * 4 + part, 1)
        return carry

    for copy in copies[0] + others:
        copy.wait()
    lax.fori_loop(0, 8, first, 0, unroll=2)

    def two(turn, carry):
        both(2 * turn + 1, 1)

        @pl.when(turn == 1)
        def _():
            for copy in copies[1]:
                copy.wait()

        both(2 * turn + 2, 0)

        @pl.when(turn == 1)
        def _():
            gather(0)

        return carry

    lax.fori_loop(0, 3, two, 0)
    both(KLOC * YS - 1, 1)
    lax.fori_loop(0, 2, last, 0)
    gather(1)

    def places_of(tile):
        return pl.ds(pl.multiple_of(tile * 256, 256), 256)

    def sent(tile):
        return [
            pltpu.make_async_copy(
                source.at[:, :, :, places_of(tile)], target.at[:, :, :, places_of(tile)], out_sems.at[tile, which]
            )
            for which, (source, target) in enumerate(((near_ref, near_hbm), (far_ref, far_hbm)))
        ]

    def one_column(tile):
        out = product(0, places_of(tile)) + product(1, places_of(tile))
        for part in range(2):
            for to in range(OWNERS):
                row = part * ROWS + to * 8
                near_ref[to, part, :, places_of(tile)] = out[row : row + 8]
                far_ref[to, part, :, places_of(tile)] = out[row + ROWS // 2 : row + ROWS // 2 + 8]
        for copy in sent(tile):
            copy.start()

    def columns_of(turn, carry):
        for part in range(2):
            one_column(turn * 2 + part)
        return carry

    def done(tile, carry):
        for copy in sent(tile):
            copy.wait()
        return carry

    lax.fori_loop(0, NG // 256 // 2, columns_of, 0)
    lax.fori_loop(0, NG // 256, done, 0)


def partial_rows(places, sym_map, rows, occ, emp, strength, level):
    whi, wlo = plane_matrices()
    vmem = pl.BlockSpec(memory_space=pltpu.VMEM)
    smem = pl.BlockSpec(memory_space=pltpu.SMEM)
    hbm = pl.BlockSpec(memory_space=pl.ANY)
    part = jax.ShapeDtypeStruct((OWNERS, 2, 8, NG), jnp.float32)
    return pl.pallas_call(
        kernel,
        out_shape=(part, part),
        in_specs=[smem, smem, smem] + [hbm] * 5 + [vmem, vmem, hbm, hbm],
        out_specs=(hbm, hbm),
        scratch_shapes=[
            pltpu.VMEM((KLOC, 2, VB, POINTS), jnp.float32),
            pltpu.VMEM((KLOC, YS, 2, 2, WIDE), jnp.float32),
            pltpu.VMEM((2, PLANE, PLANE), jnp.bfloat16),
            pltpu.VMEM((2, PLANE, PLANE), jnp.bfloat16),
            pltpu.VMEM((2, 4, 4, 2, 16, HALF), jnp.float32),
        ]
        + [pltpu.VMEM((2, GRID * CHUNK, PLANE), jnp.bfloat16)] * 4
        + [pltpu.VMEM((POINTS * 8 + 8, CHUNK), jnp.float32)]
        + [pltpu.VMEM((16 * 8 + 8, CHUNK), jnp.float32)] * 9
        + [pltpu.VMEM((NG, DEPTH), jnp.bfloat16)] * 4
        + [pltpu.VMEM((2 * ROWS, DEPTH), jnp.bfloat16)] * 4
        + [pltpu.VMEM((OWNERS, 2, 8, NG), jnp.float32)] * 2
        + [
            pltpu.VMEM((8, CHUNK), jnp.float32),
            pltpu.SMEM((KLOC * NG,), jnp.int32),
            pltpu.SemaphoreType.DMA((KLOC, 2)),
            pltpu.SemaphoreType.DMA((2 + YS,)),
            pltpu.SemaphoreType.DMA((NG // 256, 2)),
        ],
        compiler_params=pltpu.CompilerParams(vmem_limit_bytes=62 * 2**20),
        cost_estimate=pl.CostEstimate(flops=40 * 10**9, bytes_accessed=10 * 2**20, transcendentals=0),
    )(places, sym_map, rows, occ, *emp, strength, level, jnp.asarray(whi), jnp.asarray(wlo))


def shifted(value, axis, by):
    size = lax.axis_size(axis)
    return lax.ppermute(value, axis, [(index, (index + by) % size) for index in range(size)])


def local(occ_orb, occ_energy, emp_orb, emp_energy, gidx, sym_map, weights, count):
    ka = lax.axis_index(KA_AXES)
    core = lax.axis_index("core")
    y = lax.axis_index("y")
    member = lax.axis_index(("x_lo", "z"))

    spread = jnp.pad(emp_orb, ((0, 0), (0, 0), (0, 0), (0, WIDE - POINTS)))
    lane = lax.broadcasted_iota(jnp.int32, spread.shape, 3)
    lines = jnp.where(lane < POINTS, spread, emp_energy[:, :, None, None])
    own = jnp.stack([lines[1], shifted(lines[0], KA_AXES, -1)])
    emp = [own] + [shifted(own, "y", -step) for step in range(1, YS)]

    kpoint = ka * KLOC + jnp.arange(KLOC, dtype=jnp.int32)
    wrapped = (kpoint + 1 >= KA * KLOC).astype(jnp.int32)
    target = kpoint + 1 - wrapped * (KA * KLOC)
    odd = (gidx // GRID) % 2
    outer = (gidx // (2 * GRID)) % 8
    places = (gidx // PLANE * PLANE + odd * HALF + outer * GRID + gidx % GRID) * 8

    wsum = jnp.sum(weights).astype(jnp.float32)
    scale = -4.0 / jnp.sqrt(jnp.float32(VB * 2 * BAND) * wsum) / POINTS
    owner = (y + jnp.arange(YS, dtype=jnp.int32)) % YS
    bands = owner[:, None] * (2 * MEMBERS) + member * 2 + jnp.arange(2, dtype=jnp.int32)[None, :]
    live = (bands[None] < count[target][:, None, None]).astype(jnp.float32)
    strength = (scale * weights[kpoint].astype(jnp.float32))[:, None, None, None]
    strength = jnp.broadcast_to(strength * live[..., None], (KLOC, YS, 2, VB)).reshape(KLOC * YS, CHUNK)
    level = jnp.concatenate([occ_energy, occ_energy], axis=1)

    near_core = jnp.arange(2, dtype=jnp.int32)[:, None, None]
    x = lax.axis_index(("x_hi", "x_lo"))
    z = lax.axis_index("z")
    to_x = (x + jnp.arange(4, dtype=jnp.int32)[None, :, None]) % 4
    to_z = (z + jnp.arange(4, dtype=jnp.int32)[None, None, :]) % 4
    to_ka = (to_x // 2) * 2 + (core + near_core) % 2
    rows = (to_ka * 256 + y * 64 + (to_x % 2) * 32 + to_z * 8).reshape(32)
    rows = jnp.concatenate([rows, wrapped * (PLANE * 8)])

    near, far = partial_rows(places, sym_map.reshape(KLOC * NG), rows.astype(jnp.int32), occ_orb, emp, strength, level)

    both = near + shifted(far, "core", 1)
    both = both.reshape(4, 4, 2, 8, NG)
    x_axes = ("x_hi", "x_lo")

    def added(own, parts):
        return own + (parts[0] + parts[1]) + parts[2]

    first, second = both[:, :, 0], both[:, :, 1]
    first_parts = [shifted(first[:, step], "z", step) for step in range(1, 4)]
    second_parts = [shifted(second[step], x_axes, step) for step in range(1, 4)]
    first = added(first[:, 0], first_parts)
    second = added(second[0], second_parts)
    first_parts = [shifted(first[step], x_axes, step) for step in range(1, 4)]
    second_parts = [shifted(second[step], "z", step) for step in range(1, 4)]
    owned = jnp.stack([added(first[0], first_parts), added(second[0], second_parts)], axis=1)
    return owned[None]


def solution(mesh):
    fine = Mesh(mesh.devices.reshape(2, 2, YS, 2, 4), KA_AXES + BAND_AXES)
    return jax.shard_map(
        local,
        mesh=fine,
        in_specs=(
            P(KA_AXES, None, None, None),
            P(KA_AXES, None),
            P(KA_AXES, BAND_AXES, None, None),
            P(KA_AXES, BAND_AXES),
            P(),
            P(KA_AXES, None),
            P(),
            P(),
        ),
        out_specs=P(None, KA_AXES + BAND_AXES, None, None),
        check_vma=False,
    )
```
